512 devices in a mesh: dp: 32 (over z_lo, y, core), rows: 16 (over x, z_hi).
Axes of the slice: x: 4, y: 4, z: 16 (z_hi: 4, z_lo: 4; z = z_hi * 4 + z_lo), core: 2. Of those that a mesh axis runs over, the one named last changes fastest.
Arguments:
- fine_level: bfloat16 [32, 192, 48, 384], P('dp', 'rows'), may hold values from -6 to 6
- coarse_level: bfloat16 [32, 96, 24, 384], P('dp', 'rows'), may hold values from -6 to 6
- merging_weights: float32 [2], replicated, may hold values from 0.3 to 3
- depth_weight: float32 [3, 3, 384], replicated, may hold values from -2 to 2
- point_weight: bfloat16 [384, 384], replicated, may hold values from -0.3125 to 0.3125
- norm_gain: float32 [384], replicated, may hold values from 0.5 to 1.5
- cotangent: bfloat16 [32, 192, 48, 384], P('dp', 'rows'), may hold values from -48 to 48
Outputs:
- grad_fine: bfloat16 [32, 192, 48, 384], P('dp', 'rows')
- grad_coarse: bfloat16 [32, 96, 24, 384], P('dp', 'rows')
- grad_merging: float32 [2], replicated
- grad_depth: float32 [3, 3, 384], replicated
- grad_point: bfloat16 [384, 384], replicated
- grad_gain: float32 [384], replicated
- grad_shift: float32 [384], replicated
The draws below stay inside these ranges and needn't reach their ends.
All inputs are finite; a program needn't handle non-finite values.
Results may differ from the reference program's by a relative error of at most 0.02.
Values may be sent and summed in bfloat16 or wider, within the bound.
No kernel may reach another device: no remote copies, remote signals or barrier semaphores. Data moves between devices by JAX's collectives and lax.ppermute only.
A program may use at most 64 MiB of HBM per device.

```python
import math
import jax
import jax.numpy as jnp
from jax import lax

C = 384
COLS = 48
IMAGES = 32
H3 = 192


def draw_cotangent(key, part):
    key = jax.random.fold_in(key, 7)
    shape = (IMAGES, H3, COLS, C)
    first_key = jax.random.fold_in(key, 0)
    image_pos = jnp.arange(IMAGES, dtype=jnp.float32).reshape(IMAGES, 1, 1, 1)
    row_pos = jnp.arange(H3, dtype=jnp.float32).reshape(1, H3, 1, 1)
    ramp = 1.0 + 2.0 * (image_pos * H3 + row_pos) / (IMAGES * H3)
    values = jax.random.truncated_normal(first_key, -5.0, 5.0, shape, jnp.float32) * ramp
    return jnp.clip(values, -48.0, 48.0).astype(jnp.bfloat16)


def level_of(rng, extent, cuts, least, high):
    def one(position, parts):
        draws = jax.random.uniform(jax.random.fold_in(jax.random.fold_in(rng, 6), position), (parts,), jnp.float32, least / len(cuts), high / len(cuts))
        return jnp.repeat(jnp.exp(draws), extent[position] // parts).reshape((-1,) + (1,) * (len(extent) - position - 1))

    level = one(*cuts[0])
    for cut in cuts[1:]:
        level = level * one(*cut)
    return level


def noise(stream_key, dims, scale, limit, pieces=(), held_as=jnp.bfloat16):
    array = scale * jax.random.normal(stream_key, dims, jnp.float32)
    if pieces:
        array = array * level_of(stream_key, dims, pieces, -0.22, 0.18)
    return jnp.clip(array, -limit, limit).astype(held_as)


def setup_inputs(seed: int = 0) -> dict:
    arg_keys = jax.random.split(jax.random.key(seed), 8)
    return {
        "fine_level": noise(arg_keys[0], (IMAGES, H3, COLS, C), 1.0, 6.0, ((0, 32), (1, 16))),
        "coarse_level": noise(arg_keys[1], (IMAGES, H3 // 2, COLS // 2, C), 1.0, 6.0, ((0, 32), (1, 16))),
        "merging_weights": jnp.clip(jnp.exp(jax.random.uniform(arg_keys[2], (2,), jnp.float32, math.log(0.3), math.log(3.0))), 0.3, 3.0),
        "depth_weight": noise(arg_keys[3], (3, 3, C), 9 ** -0.5, 2.0, (), jnp.float32),
        "point_weight": noise(arg_keys[4], (C, C), C ** -0.5, 0.3125),
        "norm_gain": jnp.clip(1.0 + 0.1 * jax.random.normal(arg_keys[5], (C,), jnp.float32), 0.5, 1.5),
        "cotangent": draw_cotangent(jax.random.fold_in(arg_keys[7], 71), 0),
    }


def upsample(coarse):
    return jnp.repeat(jnp.repeat(coarse, 2, axis=0), 2, axis=1)

def forward_image(fine, coarse, merging_weights, depth_weight, point_weight):
    total = merging_weights[0] + merging_weights[1] + 0.0001
    upsampled = upsample(coarse).astype(jnp.float32)
    merged = (merging_weights[0] * fine.astype(jnp.float32) + merging_weights[1] * upsampled) / total
    activated = (merged * jax.nn.sigmoid(merged)).astype(jnp.bfloat16)
    height, width = (fine.shape[0], fine.shape[1])
    padded = jnp.pad(activated, ((1, 1), (1, 1), (0, 0))).astype(jnp.float32)
    depth = jnp.zeros(fine.shape, jnp.float32)
    for a in range(3):
        for b in range(3):
            depth = depth + padded[a:a + height, b:b + width] * depth_weight[a, b]
    depth = depth.astype(jnp.bfloat16)
    projected = jnp.dot(depth.reshape(-1, depth.shape[-1]), point_weight, preferred_element_type=jnp.float32)
    return (total, upsampled, merged, padded, depth, projected)

def reference(fine_level, coarse_level, merging_weights, depth_weight, point_weight, norm_gain, cotangent):
    channels = fine_level.shape[-1]

    def first(items):
        out = forward_image(items[0], items[1], merging_weights, depth_weight, point_weight)
        projected = out[5]
        return (lax.optimization_barrier(jnp.sum(projected, axis=0)), lax.optimization_barrier(jnp.sum(projected * projected, axis=0)))
    sums, squares = lax.map(first, (fine_level, coarse_level))
    count = fine_level.shape[0] * fine_level.shape[1] * fine_level.shape[2]
    mean = lax.optimization_barrier(jnp.sum(sums, axis=0)) / count
    variance = lax.optimization_barrier(jnp.sum(squares, axis=0)) / count - mean * mean
    inv_std = 1.0 / jnp.sqrt(variance + 1e-05)

    def second(items):
        out = forward_image(items[0], items[1], merging_weights, depth_weight, point_weight)
        projected = out[5]
        normed = (projected - mean) * inv_std
        grad_out = items[2].reshape(-1, channels).astype(jnp.float32)
        return (lax.optimization_barrier(jnp.sum(grad_out, axis=0)), lax.optimization_barrier(jnp.sum(grad_out * normed, axis=0)))
    shifts, gains = lax.map(second, (fine_level, coarse_level, cotangent))
    grad_shift = lax.optimization_barrier(jnp.sum(shifts, axis=0))
    grad_gain = lax.optimization_barrier(jnp.sum(gains, axis=0))

    def third(items):
        fine, coarse, grad_out = items
        total, upsampled, merged, padded, depth, projected = forward_image(fine, coarse, merging_weights, depth_weight, point_weight)
        normed = (projected - mean) * inv_std
        flat_grad = grad_out.reshape(-1, channels).astype(jnp.float32)
        grad_proj = (norm_gain * inv_std * (flat_grad - grad_shift / count - normed * grad_gain / count)).astype(jnp.bfloat16)
        flat_depth = depth.reshape(-1, channels)
        point_part = jnp.dot(flat_depth.T, grad_proj, preferred_element_type=jnp.float32)
        grad_map = jnp.dot(grad_proj, point_weight.T, preferred_element_type=jnp.float32).astype(jnp.bfloat16)
        grad_map = grad_map.reshape(fine.shape).astype(jnp.float32)
        height, width = (fine.shape[0], fine.shape[1])
        depth_part = jnp.stack([jnp.stack([lax.optimization_barrier(jnp.sum(padded[a:a + height, b:b + width] * grad_map, axis=(0, 1))) for b in range(3)]) for a in range(3)])
        padded_grad = jnp.pad(grad_map, ((1, 1), (1, 1), (0, 0)))
        grad_act = jnp.zeros(fine.shape, jnp.float32)
        for a in range(3):
            for b in range(3):
                grad_act = grad_act + padded_grad[2 - a:2 - a + height, 2 - b:2 - b + width] * depth_weight[a, b]
        sig = jax.nn.sigmoid(merged)
        grad_merged = grad_act * sig * (1.0 + merged * (1.0 - sig))
        grad_fine = (grad_merged * merging_weights[0] / total).astype(jnp.bfloat16)
        blocks = grad_merged.reshape(height // 2, 2, width // 2, 2, channels).sum(axis=(1, 3))
        grad_coarse = (blocks * merging_weights[1] / total).astype(jnp.bfloat16)
        merging_part = jnp.stack([jnp.sum(grad_merged * (fine.astype(jnp.float32) - merged) / total), jnp.sum(grad_merged * (upsampled - merged) / total)])
        return (grad_fine, grad_coarse, point_part, depth_part, merging_part)
    grad_fine, grad_coarse, point_parts, depth_parts, merging_parts = lax.map(third, (fine_level, coarse_level, cotangent))
    grad_point = lax.optimization_barrier(jnp.sum(point_parts, axis=0)).astype(jnp.bfloat16)
    grad_depth = lax.optimization_barrier(jnp.sum(depth_parts, axis=0))
    grad_merging = lax.optimization_barrier(jnp.sum(merging_parts, axis=0))
    return (grad_fine, grad_coarse, grad_merging, grad_depth, grad_point, norm_gain * 0.0 + grad_gain, grad_shift)
```

```python
import jax
import jax.numpy as jnp
from jax import lax
from jax.sharding import PartitionSpec as P

AXES = ("dp", "rows")
COUNT = 294912
bf16, f32 = jnp.bfloat16, jnp.float32


def groups_of(bits):
    rest = [b for b in range(9) if b not in bits]

    def spread(value, places):
        return sum(((value >> i) & 1) << b for i, b in enumerate(places))

    return [
        [spread(r, rest) + spread(m, bits) for m in range(1 << len(bits))]
        for r in range(1 << len(rest))
    ]


PLANE = groups_of([2, 3, 4, 5, 6])
DEPTH = groups_of([0, 1, 7, 8])


def exchange(parts, groups):
    return lax.all_to_all(parts, AXES, 0, 0, axis_index_groups=groups)


def spread_to(block, groups):
    return exchange(jnp.broadcast_to(block[None], (len(groups[0]),) + block.shape), groups)


def summed_over(block, groups):
    return jnp.sum(spread_to(block, groups), axis=0)


def two_parts(values):
    high = values.astype(bf16)
    return high, (values - high.astype(f32)).astype(bf16)


def pad_columns(field):
    return jnp.pad(field, ((0, 0), (1, 1), (0, 0)))


def on_device(
    fine_level, coarse_level, merging_weights, depth_weight, point_weight, norm_gain, cotangent
):
    fine, coarse, cot = fine_level[0], coarse_level[0], cotangent[0]
    height, width, channels = fine.shape
    half = width // 2

    def pack(fine_rows, coarse_row, cot_row):
        return jnp.concatenate([fine_rows.reshape(-1, channels), coarse_row, cot_row], axis=0)

    head = pack(fine[:2], coarse[0], cot[0])
    tail = pack(fine[-2:], coarse[-1], cot[-1])
    n = lax.axis_size("rows")
    above = lax.ppermute(tail, "rows", [(i, i + 1) for i in range(n - 1)])
    below = lax.ppermute(head, "rows", [(i + 1, i) for i in range(n - 1)])

    def unpack(packed):
        return (
            packed[: 2 * width].reshape(2, width, channels),
            packed[2 * width : 2 * width + half][None],
            packed[2 * width + half :][None],
        )

    fa, ca, ga = unpack(above)
    fb, cb, gb = unpack(below)
    fine_ext = jnp.concatenate([fa, fine, fb], axis=0).astype(f32)
    coarse_ext = jnp.concatenate([ca, coarse, cb], axis=0)
    cot_ext = jnp.concatenate([ga, cot, gb], axis=0).astype(f32)

    total = merging_weights[0] + merging_weights[1] + 0.0001
    up_ext = jnp.repeat(jnp.repeat(coarse_ext, 2, axis=0), 2, axis=1).astype(f32)
    merged_ext = (merging_weights[0] * fine_ext + merging_weights[1] * up_ext) / total
    sig_ext = jax.nn.sigmoid(merged_ext)
    act = pad_columns((merged_ext * sig_ext).astype(bf16)).astype(f32)
    rows = height + 2
    depth = jnp.zeros((rows, width, channels), f32)
    for a in range(3):
        for b in range(3):
            depth = depth + act[a : a + rows, b : b + width] * depth_weight[a, b]
    depth = depth.astype(bf16)
    projected = jnp.einsum("hwc,cd->hwd", depth, point_weight, preferred_element_type=f32)
    own = projected[1:-1]
    own_cot = cot_ext[1:-1]
    stats = jnp.stack(
        [
            jnp.sum(own, axis=(0, 1)),
            jnp.sum(own * own, axis=(0, 1)),
            jnp.sum(own_cot, axis=(0, 1)),
            jnp.sum(own_cot * own, axis=(0, 1)),
        ]
    )
    stats = summed_over(summed_over(stats.reshape(12, 128), PLANE), DEPTH).reshape(4, channels)
    mean = stats[0] / COUNT
    variance = stats[1] / COUNT - mean * mean
    inv_std = 1.0 / jnp.sqrt(variance + 1e-05)
    grad_shift = stats[2]
    grad_gain = inv_std * (stats[3] - mean * grad_shift)

    normed = (projected - mean) * inv_std
    grad_proj = (
        norm_gain * inv_std * (cot_ext - grad_shift / COUNT - normed * grad_gain / COUNT)
    ).astype(bf16)
    point_part = jnp.einsum(
        "hwc,hwd->cd", depth[1:-1], grad_proj[1:-1], preferred_element_type=f32
    )
    grad_map = jnp.einsum("hwd,cd->hwc", grad_proj, point_weight, preferred_element_type=f32)
    place = lax.axis_index("rows")
    row = jnp.arange(rows).reshape(rows, 1, 1)
    outside = ((place == 0) & (row == 0)) | ((place == n - 1) & (row == rows - 1))
    grad_map = jnp.where(outside, 0.0, grad_map).astype(bf16).astype(f32)
    own_map = grad_map[1:-1]
    depth_part = jnp.stack(
        [
            jnp.sum(act[a + 1 : a + 1 + height, b : b + width] * own_map, axis=(0, 1))
            for a in range(3)
            for b in range(3)
        ]
    )
    padded = pad_columns(grad_map)
    grad_act = jnp.zeros((height, width, channels), f32)
    for a in range(3):
        for b in range(3):
            grad_act = (
                grad_act + padded[2 - a : 2 - a + height, 2 - b : 2 - b + width] * depth_weight[a, b]
            )
    merged, sig, fine_float, up = (
        merged_ext[2:-2],
        sig_ext[2:-2],
        fine_ext[2:-2],
        up_ext[2:-2],
    )
    grad_merged = grad_act * sig * (1.0 + merged * (1.0 - sig))
    grad_fine = (grad_merged * merging_weights[0] / total).astype(bf16)
    blocks = grad_merged.reshape(height // 2, 2, half, 2, channels).sum(axis=(1, 3))
    grad_coarse = (blocks * merging_weights[1] / total).astype(bf16)
    merging_part = jnp.stack(
        [
            jnp.sum(grad_merged * (fine_float - merged) / total, axis=(0, 1)),
            jnp.sum(grad_merged * (up - merged) / total, axis=(0, 1)),
        ]
    )
    small = jnp.concatenate([depth_part, merging_part], axis=0).reshape(32, -1)
    many = small.shape[1]

    def joined(point, rest):
        return jnp.concatenate([point.astype(bf16), *two_parts(rest)], axis=-1)

    def parted(both):
        both = both.astype(f32)
        return both[..., : -2 * many], both[..., -2 * many : -many] + both[..., -many:]

    point, rest = parted(exchange(joined(point_part.reshape(32, -1), small), PLANE))
    point, rest = jnp.sum(point, axis=0), jnp.sum(rest, axis=0)
    point, rest = parted(spread_to(joined(point, rest), DEPTH))
    point, rest = jnp.sum(point, axis=0), jnp.sum(rest, axis=0)
    point, rest = parted(spread_to(joined(point, rest), PLANE))
    grad_point = point.astype(bf16).reshape(channels, channels)
    rest = rest.reshape(11, channels)
    grad_depth = rest[:9].reshape(3, 3, channels)
    grad_merging = jnp.sum(rest[9:], axis=1)
    return (
        grad_fine[None],
        grad_coarse[None],
        grad_merging,
        grad_depth,
        grad_point,
        grad_gain,
        grad_shift,
    )


def solution(mesh):
    split = P("dp", "rows", None, None)
    return jax.shard_map(
        on_device,
        mesh=mesh,
        in_specs=(split, split, P(), P(), P(), P(), split),
        out_specs=(split, split, P(), P(), P(), P(), P()),
        check_vma=False,
    )
```

```python
import jax
import jax.numpy as jnp
from jax import lax
from jax.experimental import pallas as pl
from jax.experimental.pallas import tpu as pltpu
from jax.sharding import PartitionSpec as P

AXES = ("dp", "rows")
COUNT = 294912
HEIGHT, WIDTH, CH, LANES = 12, 48, 384, 128
HALF = WIDTH // 2
MID = HEIGHT - 2
PIECE = 36
SLOT = 40
bf16, f32 = jnp.bfloat16, jnp.float32


def groups_of(bits):
    rest = [b for b in range(9) if b not in bits]

    def spread(value, places):
        return sum(((value >> i) & 1) << b for i, b in enumerate(places))

    return [
        [spread(r, rest) + spread(m, bits) for m in range(1 << len(bits))]
        for r in range(1 << len(rest))
    ]


PLANE = groups_of([2, 3, 4, 5, 6])
DEPTH = groups_of([0, 1, 7, 8])


def exchange(parts, groups):
    return lax.all_to_all(parts, AXES, 0, 0, axis_index_groups=groups)


def column():
    return lax.broadcasted_iota(jnp.int32, (WIDTH, LANES), 0)


def from_left(x):
    return jnp.where(column() == 0, 0.0, pltpu.roll(x, 1, 0))


def from_right(x):
    return jnp.where(column() == WIDTH - 1, 0.0, pltpu.roll(x, WIDTH - 1, 0))


def shares(weights):
    first, second = jnp.full((1, LANES), weights[0]), jnp.full((1, LANES), weights[1])
    total = first + second + 0.0001
    return first / total, second / total, total


def doubled(coarse):
    n = coarse.shape[0]
    row = lax.broadcasted_iota(jnp.int32, (2 * n, n), 0)
    place = lax.broadcasted_iota(jnp.int32, (2 * n, n), 1)
    pick = jnp.where((row == 2 * place) | (row == 2 * place + 1), 1.0, 0.0).astype(bf16)
    return jnp.dot(pick, coarse, preferred_element_type=f32)


def blocks():
    return [slice(c * LANES, (c + 1) * LANES) for c in range(CH // LANES)]


def activate(fine, up, share):
    merged = share[0] * fine + share[1] * up
    sig = jax.nn.sigmoid(merged)
    return merged, sig, (merged * sig).astype(bf16).astype(f32)


def convolve(act, i, dw, c):
    rows = [act[i + a - 1, :, c] for a in range(3)]
    across = [sum(rows[a] * dw[a, b : b + 1, c] for a in range(3)) for b in range(3)]
    return from_left(across[0]) + across[1] + from_right(across[2])


def folded(x):
    return jnp.sum(x.reshape(-1, 8, x.shape[-1]), axis=0)


def statistics(proj, cot):
    parts = (proj, proj * proj, cot, cot * proj)
    return [jnp.sum(folded(p), axis=0, keepdims=True) for p in parts]


def pack_kernel(ft, fb, ct, cb, gt, gb, head, tail):
    n = 2 * WIDTH
    for out, fine, coarse, cot in ((head, ft, ct, gt), (tail, fb, cb, gb)):
        out[0:WIDTH] = fine[0, 0]
        out[WIDTH:n] = fine[0, 1]
        out[n : n + WIDTH] = cot[0, 0]
        out[n + WIDTH : n + WIDTH + HALF] = coarse[0, 0]


def middle_kernel(mw, fine, coarse, dw, pw, cot, depth, proj, stats, act, up):
    share = shares(mw)
    up[...] = doubled(coarse[0].reshape(-1, CH))
    for c in blocks():
        for i in range(HEIGHT):
            u = up[(i // 2) * WIDTH : (i // 2 + 1) * WIDTH, c]
            act[i, :, c] = activate(fine[0, i, :, c].astype(f32), u, share)[2]
        for i in range(1, HEIGHT - 1):
            depth[(i - 1) * WIDTH : i * WIDTH, c] = convolve(act, i, dw, c).astype(bf16)
    proj[...] = jnp.dot(depth[...], pw[...], preferred_element_type=f32)
    own = cot[0, 1 : HEIGHT - 1].reshape(-1, CH).astype(f32)
    for k, s in enumerate(statistics(proj[...], own)):
        stats[k : k + 1] = s


def edge_kernel(mw, above, below, ft, fb, ct, cb, gt, gb, dw, pw, mid, depth, proj, stats, act):
    share = shares(mw)
    n = 2 * WIDTH
    for e in range(2):
        halo, fine, coarse = (above, ft, ct) if e == 0 else (below, fb, cb)
        far = doubled(halo[n + WIDTH : n + WIDTH + HALF])
        near = doubled(coarse[0, 0])
        for c in blocks():
            for r in range(2):
                h, o = (r, r + 2) if e == 0 else (r + 2, r)
                outer = halo[r * WIDTH : (r + 1) * WIDTH, c].astype(f32)
                act[e, h, :, c] = activate(outer, far[:, c], share)[2]
                act[e, o, :, c] = activate(fine[0, r, :, c].astype(f32), near[:, c], share)[2]
            for r in range(2):
                at = (2 * e + r) * WIDTH
                depth[at : at + WIDTH, c] = convolve(act.at[e], r + 1, dw, c).astype(bf16)
    proj[...] = jnp.dot(depth[...], pw[...], preferred_element_type=f32)
    first = statistics(proj[WIDTH : 2 * WIDTH], gt[0, 0].astype(f32))
    last = statistics(proj[2 * WIDTH : 3 * WIDTH], gb[0, 0].astype(f32))
    whole = jnp.concatenate([x + y for x, y in zip(first, last)], axis=0) + mid[...]
    stats[...] = jnp.broadcast_to(whole[None], stats.shape)


def total_kernel(parts, out):
    out[...] = jnp.broadcast_to(jnp.sum(parts[...], axis=0)[None], out.shape)


def backward_kernel(
    mw, gathered, above, below, fine, coarse, dw, pw, gain, cot, depth_mid, depth_edge,
    proj_mid, proj_edge, grad_fine, grad_coarse, send, grad_gain, grad_shift,
    own_depth, gproj, gmap, up, pairs, point, slots,
):
    share = shares(mw)
    n = 2 * WIDTH
    stats = jnp.sum(gathered[...], axis=0)
    mean = stats[0:1] / COUNT
    variance = stats[1:2] / COUNT - mean * mean
    inv_std = 1.0 / jnp.sqrt(variance + 1e-05)
    shift = stats[2:3]
    gained = inv_std * (stats[3:4] - mean * shift)
    grad_gain[...] = gained
    grad_shift[...] = shift
    scale = gain[...] * inv_std
    by_proj = -(scale * inv_std * gained) / COUNT
    offset = -(scale * shift) / COUNT

    def gradient(g, p):
        return (scale * g.astype(f32) + (by_proj * (p - mean) + offset)).astype(bf16)

    end = HEIGHT * WIDTH
    gproj[0:WIDTH] = gradient(above[n : n + WIDTH], proj_edge[0:WIDTH])
    gproj[WIDTH:n] = gradient(cot[0, 0], proj_edge[WIDTH:n])
    mid_cot = cot[0, 1 : HEIGHT - 1].reshape(-1, CH)
    gproj[n : end] = gradient(mid_cot, proj_mid[...])
    gproj[end : end + WIDTH] = gradient(cot[0, HEIGHT - 1], proj_edge[n : n + WIDTH])
    gproj[end + WIDTH : end + n] = gradient(below[n : n + WIDTH], proj_edge[n + WIDTH : 2 * n])
    own_depth[0:WIDTH] = depth_edge[WIDTH:n]
    own_depth[WIDTH : end - WIDTH] = depth_mid[...]
    own_depth[end - WIDTH : end] = depth_edge[n : n + WIDTH]
    at_place = lax.axis_index("rows")
    keep = (
        jnp.where(at_place == 0, 0.0, 1.0),
        jnp.where(at_place == lax.axis_size("rows") - 1, 0.0, 1.0),
    )
    whole_map = lax.dot_general(
        gproj[...], pw[...], (((1,), (1,)), ((), ())), preferred_element_type=f32
    ).astype(bf16).astype(f32)
    whole_point = lax.dot_general(
        own_depth[...], gproj[WIDTH : end + WIDTH], (((0,), (0,)), ((), ())),
        preferred_element_type=f32,
    )
    for k, c in enumerate(blocks()):
        point[k * CH : (k + 1) * CH] = whole_point[:, c]
        for r in range(HEIGHT + 2):
            x = whole_map[r * WIDTH : (r + 1) * WIDTH, c]
            if r == 0:
                x = x * keep[0]
            if r == HEIGHT + 1:
                x = x * keep[1]
            gmap[0, r, :, c] = from_right(x)
            gmap[1, r, :, c] = x
            gmap[2, r, :, c] = from_left(x)
    up[...] = doubled(coarse[0].reshape(-1, CH))
    by_weight = [jnp.zeros((8, LANES), f32)] * 2
    zero = jnp.zeros((1, LANES), f32)
    small = [zero] * 32
    for k, c in enumerate(blocks()):
        taps = [jnp.zeros((8, LANES), f32)] * 9
        for p in range(HEIGHT):
            fine_row = fine[0, p, :, c].astype(f32)
            u = up[(p // 2) * WIDTH : (p // 2 + 1) * WIDTH, c]
            merged, sig, act = activate(fine_row, u, share)
            grad_act = jnp.zeros((WIDTH, LANES), f32)
            for a in range(3):
                for b in range(3):
                    x = gmap[b, p + 2 - a, :, c]
                    grad_act = grad_act + x * dw[a, b : b + 1, c]
                    taps[3 * a + b] = taps[3 * a + b] + folded(act * x)
            grad_merged = grad_act * (sig * (1.0 + merged * (1.0 - sig)))
            grad_fine[0, p, :, c] = (grad_merged * share[0]).astype(bf16)
            by_weight[0] = by_weight[0] + folded(grad_merged * (fine_row - merged))
            by_weight[1] = by_weight[1] + folded(grad_merged * (u - merged))
            at = k * HEIGHT * HALF + (p // 2) * WIDTH
            if p % 2 == 0:
                pairs[at : at + WIDTH] = grad_merged
            else:
                pairs[at : at + WIDTH] = pairs[at : at + WIDTH] + grad_merged
        for t in range(9):
            small[3 * t + k] = jnp.sum(taps[t], axis=0, keepdims=True)
    for t in range(2):
        small[27 + t] = jnp.sum(by_weight[t], axis=0, keepdims=True) / share[2]
    m = HEIGHT * HALF // 2
    for k, c in enumerate(blocks()):
        both = pairs[pl.ds(2 * k * m, m, stride=2)] + pairs[pl.ds(2 * k * m + 1, m, stride=2)]
        grad_coarse[0, :, :, c] = (both * share[1]).astype(bf16).reshape(HEIGHT // 2, HALF, LANES)
    for s in range(32):
        slots[s, 0:PIECE] = point[s * PIECE : (s + 1) * PIECE]
        high = small[s].astype(bf16).astype(f32)
        slots[s, PIECE:SLOT] = jnp.concatenate([high, small[s] - high, zero, zero], axis=0)
    send[...] = slots[...].astype(bf16)


def relay_kernel(parts, out):
    total = jnp.sum(parts[...].astype(f32), axis=0)
    value = total[PIECE : PIECE + 1] + total[PIECE + 1 : PIECE + 2]
    high = value.astype(bf16).astype(f32)
    row = lax.broadcasted_iota(jnp.int32, (SLOT, LANES), 0)
    total = jnp.where(row == PIECE, high, jnp.where(row == PIECE + 1, value - high, total))
    out[...] = jnp.broadcast_to(total.astype(bf16)[None], out.shape)


def finish_kernel(parts, grad_point, grad_depth, grad_merging, point):
    rest = []
    for s in range(32):
        slot = parts[s].astype(f32)
        point[s * PIECE : (s + 1) * PIECE] = slot[0:PIECE]
        rest.append(slot[PIECE : PIECE + 1] + slot[PIECE + 1 : PIECE + 2])
    for k, c in enumerate(blocks()):
        grad_point[:, c] = point[k * CH : (k + 1) * CH].astype(bf16)
        for t in range(9):
            grad_depth[t // 3, t % 3 : t % 3 + 1, c] = rest[3 * t + k]
    sums = [jnp.sum(rest[27 + t], axis=1, keepdims=True) for t in range(2)]
    grad_merging[...] = jnp.concatenate(sums, axis=1)


VMEM = pl.BlockSpec(memory_space=pltpu.VMEM)
SMEM = pl.BlockSpec(memory_space=pltpu.SMEM)


def call(kernel, name, outs, scratch=(), in_specs=None, cost=0, grid=()):
    return pl.pallas_call(
        kernel,
        name=name,
        grid=grid,
        out_shape=[jax.ShapeDtypeStruct(s, t) for s, t in outs],
        in_specs=in_specs or [VMEM],
        out_specs=[VMEM] * len(outs),
        scratch_shapes=[pltpu.VMEM(s, t) for s, t in scratch],
        compiler_params=pltpu.CompilerParams(vmem_limit_bytes=32 * 1024 * 1024),
        cost_estimate=pl.CostEstimate(flops=cost, bytes_accessed=1 << 20, transcendentals=0),
    )


def edge_specs():
    def at(shape, row):
        return pl.BlockSpec(shape, lambda i: (0, row, 0, 0))

    fine, coarse, cot = (1, 2, WIDTH, CH), (1, 1, HALF, CH), (1, 1, WIDTH, CH)
    return [
        at(fine, 0), at(fine, HEIGHT // 2 - 1), at(coarse, 0), at(coarse, HEIGHT // 2 - 1),
        at(cot, 0), at(cot, HEIGHT - 1),
    ]


def on_device(
    fine_level, coarse_level, merging_weights, depth_weight, point_weight, norm_gain, cotangent
):
    ends = (fine_level, fine_level, coarse_level, coarse_level, cotangent, cotangent)
    packed = (3 * WIDTH + HALF, CH)
    head, tail = call(pack_kernel, "pack", [(packed, bf16)] * 2, in_specs=edge_specs(), grid=(1,))(
        *ends
    )
    n = lax.axis_size("rows")
    above = lax.ppermute(tail, "rows", [(i, i + 1) for i in range(n - 1)])
    below = lax.ppermute(head, "rows", [(i + 1, i) for i in range(n - 1)])
    depth_mid, proj_mid, mid = call(
        middle_kernel,
        "middle",
        [((MID * WIDTH, CH), bf16), ((MID * WIDTH, CH), f32), ((4, CH), f32)],
        [((HEIGHT, WIDTH, CH), f32), ((HEIGHT * HALF, CH), f32)],
        [SMEM] + [VMEM] * 5,
        cost=1 << 28,
    )(merging_weights, fine_level, coarse_level, depth_weight, point_weight, cotangent)
    depth_edge, proj_edge, stats = call(
        edge_kernel,
        "edge",
        [((4 * WIDTH, CH), bf16), ((4 * WIDTH, CH), f32), ((32, 4, CH), f32)],
        [((2, 4, WIDTH, CH), f32)],
        [SMEM, VMEM, VMEM] + edge_specs() + [VMEM] * 3,
        grid=(1,),
    )(merging_weights, above, below, *ends, depth_weight, point_weight, mid)
    (stats,) = call(total_kernel, "statistics", [((16, 4, CH), f32)])(exchange(stats, PLANE))
    stats = exchange(stats, DEPTH)
    grad_fine, grad_coarse, send, grad_gain, grad_shift = call(
        backward_kernel,
        "backward",
        [
            (fine_level.shape, bf16),
            (coarse_level.shape, bf16),
            ((32, SLOT, LANES), bf16),
            ((1, CH), f32),
            ((1, CH), f32),
        ],
        [
            ((HEIGHT * WIDTH, CH), bf16),
            (((HEIGHT + 2) * WIDTH, CH), bf16),
            ((3, HEIGHT + 2, WIDTH, CH), f32),
            ((HEIGHT * HALF, CH), f32),
            ((3 * HEIGHT * HALF, LANES), f32),
            ((3 * CH, LANES), f32),
            ((32, SLOT, LANES), f32),
        ],
        [SMEM] + [VMEM] * 13,
    )(
        merging_weights, stats, above, below, fine_level, coarse_level, depth_weight, point_weight,
        norm_gain.reshape(1, CH), cotangent, depth_mid, depth_edge, proj_mid, proj_edge,
    )
    (part,) = call(relay_kernel, "sum_plane", [((16, SLOT, LANES), bf16)])(exchange(send, PLANE))
    (part,) = call(relay_kernel, "sum_depth", [((32, SLOT, LANES), bf16)])(exchange(part, DEPTH))
    grad_point, grad_depth, grad_merging = call(
        finish_kernel,
        "finish",
        [((CH, CH), bf16), ((3, 3, CH), f32), ((1, 2), f32)],
        [((3 * CH, LANES), f32)],
    )(exchange(part, PLANE))
    return (
        grad_fine,
        grad_coarse,
        grad_merging.reshape(2),
        grad_depth,
        grad_point,
        grad_gain.reshape(CH),
        grad_shift.reshape(CH),
    )


def solution(mesh):
    split = P("dp", "rows", None, None)
    return jax.shard_map(
        on_device,
        mesh=mesh,
        in_specs=(split, split, P(), P(), P(), P(), split),
        out_specs=(split, split, P(), P(), P(), P(), P()),
        check_vma=False,
    )
```

```python
import jax
import jax.numpy as jnp
from jax import lax
from jax.experimental import pallas as pl
from jax.experimental.pallas import tpu as pltpu
from jax.sharding import PartitionSpec as P

AXES = ("dp", "rows")
COUNT = 294912
HEIGHT, WIDTH, CH, LANES = 12, 48, 384, 128
HALF = WIDTH // 2
MID = HEIGHT - 2
PIECE = 36
SLOT = 40
bf16, f32 = jnp.bfloat16, jnp.float32


def groups_of(bits):
    rest = [b for b in range(9) if b not in bits]

    def spread(value, places):
        return sum(((value >> i) & 1) << b for i, b in enumerate(places))

    return [
        [spread(r, rest) + spread(m, bits) for m in range(1 << len(bits))]
        for r in range(1 << len(rest))
    ]


PLANE = groups_of([2, 3, 4, 5, 6])
DEPTH = groups_of([0, 1, 7, 8])


def exchange(parts, groups):
    return lax.all_to_all(parts, AXES, 0, 0, axis_index_groups=groups)


def column():
    return lax.broadcasted_iota(jnp.int32, (WIDTH, LANES), 0)


def from_left(x):
    return jnp.where(column() == 0, 0.0, pltpu.roll(x, 1, 0))


def from_right(x):
    return jnp.where(column() == WIDTH - 1, 0.0, pltpu.roll(x, WIDTH - 1, 0))


def shares(weights):
    first, second = jnp.full((1, LANES), weights[0]), jnp.full((1, LANES), weights[1])
    total = first + second + 0.0001
    return first / total, second / total, total


def doubled(coarse):
    n = coarse.shape[0]
    row = lax.broadcasted_iota(jnp.int32, (2 * n, n), 0)
    place = lax.broadcasted_iota(jnp.int32, (2 * n, n), 1)
    pick = jnp.where((row == 2 * place) | (row == 2 * place + 1), 1.0, 0.0).astype(bf16)
    return jnp.dot(pick, coarse, preferred_element_type=f32)


def blocks():
    return [slice(c * LANES, (c + 1) * LANES) for c in range(CH // LANES)]


def activate(fine, up, share):
    merged = share[0] * fine + share[1] * up
    sig = jax.nn.sigmoid(merged)
    return merged, sig, (merged * sig).astype(bf16).astype(f32)


def convolve(rows, taps, dw, c):
    across = [sum(row * dw[a, b : b + 1, c] for row, a in zip(rows, taps)) for b in range(3)]
    return from_left(across[0]) + across[1] + from_right(across[2])


def folded(x):
    return jnp.sum(x.reshape(-1, 8, x.shape[-1]), axis=0)


def statistics(proj, cot):
    parts = (proj, proj * proj, cot, cot * proj)
    return [jnp.sum(folded(p), axis=0, keepdims=True) for p in parts]


def pack_kernel(mw, ft, fb, ct, cb, gt, gb, head, tail):
    share = shares(mw)
    for out, fine, coarse, cot, rows in ((head, ft, ct, gt, (0, 1)), (tail, fb, cb, gb, (1, 0))):
        up = doubled(coarse[0, 0])
        for k, r in enumerate(rows):
            for c in blocks():
                act = activate(fine[0, r, :, c].astype(f32), up[:, c], share)[2]
                out[k * WIDTH : (k + 1) * WIDTH, c] = act.astype(bf16)
        out[2 * WIDTH : 3 * WIDTH] = cot[0, 0]


def factors(row, up, share):
    merged, sig, act = activate(row, up, share)
    slope = sig * (1.0 + merged * (1.0 - sig))
    return act, slope, ((row - merged) / share[2], (up - merged) / share[2])


def middle_kernel(
    mw, fine, coarse, dw, pw, cot, depth, proj, stats, partial, act, factor, slope, up
):
    share = shares(mw)
    up[...] = doubled(coarse[0].reshape(-1, CH))
    last = HEIGHT - 1
    for c in blocks():
        for i in range(HEIGHT):
            u = up[(i // 2) * WIDTH : (i // 2 + 1) * WIDTH, c]
            found = factors(fine[0, i, :, c].astype(f32), u, share)
            act[i, :, c], slope[i, :, c], (factor[0, i, :, c], factor[1, i, :, c]) = found
        for i in range(HEIGHT):
            taps = [a for a in range(3) if 0 <= i + a - 1 <= last]
            sums = convolve([act[i + a - 1, :, c] for a in taps], taps, dw, c)
            if 0 < i < last:
                depth[(i - 1) * WIDTH : i * WIDTH, c] = sums.astype(bf16)
            else:
                partial[i // last, :, c] = sums
    proj[...] = jnp.dot(depth[...], pw[...], preferred_element_type=f32)
    own = cot[0, 1:last].reshape(-1, CH).astype(f32)
    for k, s in enumerate(statistics(proj[...], own)):
        stats[k : k + 1] = s


def edge_kernel(above, below, partial, act, gt, gb, dw, pw, mid, depth, proj, stats):
    for e, (halo, a) in enumerate(((above, 0), (below, 2))):
        for c in blocks():
            near = halo[0:WIDTH, c].astype(f32)
            far = halo[WIDTH : 2 * WIDTH, c].astype(f32)
            inner = partial[e, :, c] + convolve((near,), (a,), dw, c)
            rows = (far, near, act[0, :, c]) if e == 0 else (act[HEIGHT - 1, :, c], near, far)
            outer = convolve(rows, range(3), dw, c)
            for k, row in enumerate((outer, inner) if e == 0 else (inner, outer)):
                at = (2 * e + k) * WIDTH
                depth[at : at + WIDTH, c] = row.astype(bf16)
    proj[...] = jnp.dot(depth[...], pw[...], preferred_element_type=f32)
    first = statistics(proj[WIDTH : 2 * WIDTH], gt[0, 0].astype(f32))
    last = statistics(proj[2 * WIDTH : 3 * WIDTH], gb[0, 0].astype(f32))
    whole = jnp.concatenate([x + y for x, y in zip(first, last)], axis=0) + mid[...]
    stats[...] = jnp.broadcast_to(whole[None], stats.shape)


def total_kernel(parts, out):
    out[...] = jnp.broadcast_to(jnp.sum(parts[...], axis=0)[None], out.shape)


def gradient_kernel(
    gathered, above, below, cot, pw, gain, depth_mid, depth_edge, proj_mid, proj_edge, act,
    send, grad_gain, grad_shift, gmap, own_depth, gproj, point, slots,
):
    n, end = 2 * WIDTH, HEIGHT * WIDTH
    stats = jnp.sum(gathered[...], axis=0)
    mean = stats[0:1] / COUNT
    variance = stats[1:2] / COUNT - mean * mean
    inv_std = 1.0 / jnp.sqrt(variance + 1e-05)
    shift = stats[2:3]
    gained = inv_std * (stats[3:4] - mean * shift)
    grad_gain[...] = gained
    grad_shift[...] = shift
    scale = gain[...] * inv_std
    by_proj = -(scale * inv_std * gained) / COUNT
    offset = -(scale * shift) / COUNT

    def gradient(g, p):
        return (scale * g.astype(f32) + (by_proj * (p - mean) + offset)).astype(bf16)

    gproj[0:WIDTH] = gradient(above[n : n + WIDTH], proj_edge[0:WIDTH])
    gproj[WIDTH:n] = gradient(cot[0, 0], proj_edge[WIDTH:n])
    mid_cot = cot[0, 1 : HEIGHT - 1].reshape(-1, CH)
    gproj[n:end] = gradient(mid_cot, proj_mid[...])
    gproj[end : end + WIDTH] = gradient(cot[0, HEIGHT - 1], proj_edge[n : n + WIDTH])
    gproj[end + WIDTH : end + n] = gradient(below[n : n + WIDTH], proj_edge[n + WIDTH : 2 * n])
    own_depth[0:WIDTH] = depth_edge[WIDTH:n]
    own_depth[WIDTH : end - WIDTH] = depth_mid[...]
    own_depth[end - WIDTH : end] = depth_edge[n : n + WIDTH]
    gmap[...] = lax.dot_general(
        gproj[...], pw[...], (((1,), (1,)), ((), ())), preferred_element_type=f32
    ).astype(bf16)
    whole_point = lax.dot_general(
        own_depth[...], gproj[WIDTH : end + WIDTH], (((0,), (0,)), ((), ())),
        preferred_element_type=f32,
    )
    zero = jnp.zeros((1, LANES), f32)
    small = [zero] * 32
    for k, c in enumerate(blocks()):
        point[k * CH : (k + 1) * CH] = whole_point[:, c]
        taps = [jnp.zeros((8, LANES), f32)] * 9
        ends = [halo[0:WIDTH, c].astype(f32) for halo in (above, below)]
        for i in range(HEIGHT):
            x = gmap[(i + 1) * WIDTH : (i + 2) * WIDTH, c].astype(f32)
            moved = from_right(x), x, from_left(x)
            for a in range(3):
                r = i + a - 1
                row = ends[0] if r < 0 else ends[1] if r == HEIGHT else act[r, :, c]
                for b in range(3):
                    taps[3 * a + b] = taps[3 * a + b] + folded(row * moved[b])
        for t in range(9):
            small[3 * t + k] = jnp.sum(taps[t], axis=0, keepdims=True)
    for s in range(32):
        slots[s, 0:PIECE] = point[s * PIECE : (s + 1) * PIECE]
        high = small[s].astype(bf16).astype(f32)
        slots[s, PIECE:SLOT] = jnp.concatenate([high, small[s] - high, zero, zero], axis=0)
    send[...] = slots[...].astype(bf16)


def level_kernel(
    mw, gmap, slope, factor, dw, grad_fine, grad_coarse, merging, moved, pairs
):
    share = shares(mw)
    m = HEIGHT * HALF // 2
    place = lax.axis_index("rows")
    keep = {
        0: jnp.where(place == 0, 0.0, 1.0),
        HEIGHT + 1: jnp.where(place == lax.axis_size("rows") - 1, 0.0, 1.0),
    }
    by_weight = [jnp.zeros((8, LANES), f32)] * 2
    for k, c in enumerate(blocks()):
        for r in range(HEIGHT + 2):
            x = gmap[r * WIDTH : (r + 1) * WIDTH, c].astype(f32)
            x = x * keep[r] if r in keep else x
            moved[0, r, :, c] = from_right(x)
            moved[1, r, :, c] = x
            moved[2, r, :, c] = from_left(x)
        for p in range(HEIGHT):
            grad_act = jnp.zeros((WIDTH, LANES), f32)
            for a in range(3):
                for b in range(3):
                    grad_act = grad_act + moved[b, p + 2 - a, :, c] * dw[a, b : b + 1, c]
            grad_merged = grad_act * slope[p, :, c]
            for t in range(2):
                by_weight[t] = by_weight[t] + folded(grad_merged * factor[t, p, :, c])
            grad_fine[0, p, :, c] = (grad_merged * share[0]).astype(bf16)
            at = 2 * k * m + (p // 2) * WIDTH
            if p % 2 == 0:
                pairs[at : at + WIDTH] = grad_merged
            else:
                pairs[at : at + WIDTH] = pairs[at : at + WIDTH] + grad_merged
        both = pairs[pl.ds(2 * k * m, m, stride=2)] + pairs[pl.ds(2 * k * m + 1, m, stride=2)]
        grad_coarse[0, :, :, c] = (both * share[1]).astype(bf16).reshape(HEIGHT // 2, HALF, LANES)
    lane = lax.broadcasted_iota(jnp.int32, (1, LANES), 1)
    first, second = [
        jnp.sum(jnp.sum(x, axis=0, keepdims=True), axis=1, keepdims=True) for x in by_weight
    ]
    merging[...] = jnp.where(lane == 0, first, jnp.where(lane == 1, second, 0.0))


def relay_kernel(parts, *refs):
    out = refs[-1]
    total = jnp.sum(parts[...].astype(f32), axis=0)
    row = lax.broadcasted_iota(jnp.int32, (SLOT, LANES), 0)
    for at in (PIECE, PIECE + 2):
        value = total[at : at + 1] + total[at + 1 : at + 2]
        if at > PIECE and len(refs) > 1:
            value = refs[0][...]
        high = value.astype(bf16).astype(f32)
        total = jnp.where(row == at, high, jnp.where(row == at + 1, value - high, total))
    out[...] = jnp.broadcast_to(total.astype(bf16)[None], out.shape)


def finish_kernel(parts, grad_point, grad_depth, grad_merging, point):
    rest, merging = [], jnp.zeros((1, LANES), f32)
    for s in range(32):
        slot = parts[s].astype(f32)
        point[s * PIECE : (s + 1) * PIECE] = slot[0:PIECE]
        rest.append(slot[PIECE : PIECE + 1] + slot[PIECE + 1 : PIECE + 2])
        merging = merging + (slot[PIECE + 2 : PIECE + 3] + slot[PIECE + 3 : PIECE + 4])
    for k, c in enumerate(blocks()):
        grad_point[:, c] = point[k * CH : (k + 1) * CH].astype(bf16)
        for t in range(9):
            grad_depth[t // 3, t % 3 : t % 3 + 1, c] = rest[3 * t + k]
    grad_merging[...] = merging[:, 0:2]


VMEM = pl.BlockSpec(memory_space=pltpu.VMEM)
SMEM = pl.BlockSpec(memory_space=pltpu.SMEM)


def call(kernel, name, outs, scratch=(), in_specs=None, cost=0, grid=(), limit=32):
    return pl.pallas_call(
        kernel,
        name=name,
        grid=grid,
        out_shape=[jax.ShapeDtypeStruct(s, t) for s, t in outs],
        in_specs=in_specs or [VMEM],
        out_specs=[VMEM] * len(outs),
        scratch_shapes=[pltpu.VMEM(s, t) for s, t in scratch],
        compiler_params=pltpu.CompilerParams(vmem_limit_bytes=limit << 20),
        cost_estimate=pl.CostEstimate(flops=cost, bytes_accessed=1 << 20, transcendentals=0),
    )


def at(shape, row):
    return pl.BlockSpec(shape, lambda i: (0, row, 0, 0))


FINE, COARSE, COT = (1, 2, WIDTH, CH), (1, 1, HALF, CH), (1, 1, WIDTH, CH)
COT_ENDS = [at(COT, 0), at(COT, HEIGHT - 1)]
FINE_ENDS = [at(FINE, 0), at(FINE, HEIGHT // 2 - 1)]
COARSE_ENDS = [at(COARSE, 0), at(COARSE, HEIGHT // 2 - 1)]


def on_device(
    fine_level, coarse_level, merging_weights, depth_weight, point_weight, norm_gain, cotangent
):
    ends = (fine_level, fine_level, coarse_level, coarse_level, cotangent, cotangent)
    head, tail = call(
        pack_kernel,
        "pack",
        [((3 * WIDTH, CH), bf16)] * 2,
        in_specs=[SMEM] + FINE_ENDS + COARSE_ENDS + COT_ENDS,
        grid=(1,),
        limit=56,
    )(merging_weights, *ends)
    n = lax.axis_size("rows")
    above = lax.ppermute(tail, "rows", [(i, i + 1) for i in range(n - 1)])
    below = lax.ppermute(head, "rows", [(i + 1, i) for i in range(n - 1)])
    whole = ((HEIGHT, WIDTH, CH), f32)
    depth_mid, proj_mid, mid, partial, act, factor, slope = call(
        middle_kernel,
        "middle",
        [
            ((MID * WIDTH, CH), bf16),
            ((MID * WIDTH, CH), f32),
            ((4, CH), f32),
            ((2, WIDTH, CH), f32),
            whole,
            ((2,) + whole[0], f32),
            whole,
        ],
        [((HEIGHT * HALF, CH), f32)],
        [SMEM] + [VMEM] * 5,
        cost=1 << 28,
    )(merging_weights, fine_level, coarse_level, depth_weight, point_weight, cotangent)
    depth_edge, proj_edge, stats = call(
        edge_kernel,
        "edge",
        [((4 * WIDTH, CH), bf16), ((4 * WIDTH, CH), f32), ((32, 4, CH), f32)],
        [],
        [VMEM] * 4 + COT_ENDS + [VMEM] * 3,
        grid=(1,),
    )(above, below, partial, act, cotangent, cotangent, depth_weight, point_weight, mid)
    (stats,) = call(total_kernel, "statistics", [((16, 4, CH), f32)])(exchange(stats, PLANE))
    send, grad_gain, grad_shift, gmap = call(
        gradient_kernel,
        "gradient",
        [
            ((32, SLOT, LANES), bf16),
            ((1, CH), f32),
            ((1, CH), f32),
            (((HEIGHT + 2) * WIDTH, CH), bf16),
        ],
        [
            ((HEIGHT * WIDTH, CH), bf16),
            (((HEIGHT + 2) * WIDTH, CH), bf16),
            ((3 * CH, LANES), f32),
            ((32, SLOT, LANES), f32),
        ],
        [VMEM] * 11,
    )(
        exchange(stats, DEPTH), above, below, cotangent, point_weight, norm_gain.reshape(1, CH),
        depth_mid, depth_edge, proj_mid, proj_edge, act,
    )
    grad_fine, grad_coarse, merging = call(
        level_kernel,
        "levels",
        [(fine_level.shape, bf16), (coarse_level.shape, bf16), ((1, LANES), f32)],
        [((3, HEIGHT + 2, WIDTH, CH), f32), ((3 * HEIGHT * HALF, LANES), f32)],
        [SMEM] + [VMEM] * 4,
        cost=1 << 28,
        limit=56,
    )(merging_weights, gmap, slope, factor, depth_weight)
    (part,) = call(
        relay_kernel, "sum_plane", [((16, SLOT, LANES), bf16)], in_specs=[VMEM] * 2
    )(exchange(send, PLANE), merging)
    (part,) = call(relay_kernel, "sum_depth", [((32, SLOT, LANES), bf16)])(exchange(part, DEPTH))
    grad_point, grad_depth, grad_merging = call(
        finish_kernel,
        "finish",
        [((CH, CH), bf16), ((3, 3, CH), f32), ((1, 2), f32)],
        [((3 * CH, LANES), f32)],
    )(exchange(part, PLANE))
    return (
        grad_fine,
        grad_coarse,
        grad_merging.reshape(2),
        grad_depth,
        grad_point,
        grad_gain.reshape(CH),
        grad_shift.reshape(CH),
    )


def solution(mesh):
    split = P("dp", "rows", None, None)
    return jax.shard_map(
        on_device,
        mesh=mesh,
        in_specs=(split, split, P(), P(), P(), P(), split),
        out_specs=(split, split, P(), P(), P(), P(), P()),
        check_vma=False,
    )
```

```python
import jax
import jax.numpy as jnp
from jax import lax
from jax.experimental import pallas as pl
from jax.experimental.pallas import tpu as pltpu
from jax.sharding import PartitionSpec as P

AXES = ("dp", "rows")
COUNT = 294912
HEIGHT, WIDTH, CH, LANES = 12, 48, 384, 128
HALF = WIDTH // 2
MID = HEIGHT - 2
PIECE = 36
SLOT = 40
bf16, f32 = jnp.bfloat16, jnp.float32


def groups_of(bits):
    rest = [b for b in range(9) if b not in bits]

    def spread(value, places):
        return sum(((value >> i) & 1) << b for i, b in enumerate(places))

    return [
        [spread(r, rest) + spread(m, bits) for m in range(1 << len(bits))]
        for r in range(1 << len(rest))
    ]


PLANE = groups_of([2, 3, 4, 5, 6])
DEPTH = groups_of([0, 1, 7, 8])


def exchange(parts, groups):
    return lax.all_to_all(parts, AXES, 0, 0, axis_index_groups=groups)


def column():
    return lax.broadcasted_iota(jnp.int32, (WIDTH, LANES), 0)


def from_left(x):
    return jnp.where(column() == 0, 0.0, pltpu.roll(x, 1, 0))


def from_right(x):
    return jnp.where(column() == WIDTH - 1, 0.0, pltpu.roll(x, WIDTH - 1, 0))


def shares(weights):
    first, second = jnp.full((1, LANES), weights[0]), jnp.full((1, LANES), weights[1])
    total = first + second + 0.0001
    return first / total, second / total, total


def doubled(coarse):
    n = coarse.shape[0]
    row = lax.broadcasted_iota(jnp.int32, (2 * n, n), 0)
    place = lax.broadcasted_iota(jnp.int32, (2 * n, n), 1)
    pick = jnp.where((row == 2 * place) | (row == 2 * place + 1), 1.0, 0.0).astype(bf16)
    return jnp.dot(pick, coarse, preferred_element_type=f32)


def blocks():
    return [slice(c * LANES, (c + 1) * LANES) for c in range(CH // LANES)]


def activate(fine, up, share):
    merged = share[0] * fine + share[1] * up
    sig = jax.nn.sigmoid(merged)
    return merged, sig, (merged * sig).astype(bf16).astype(f32)


def convolve(rows, taps, dw, c):
    across = [sum(row * dw[a, b : b + 1, c] for row, a in zip(rows, taps)) for b in range(3)]
    return from_left(across[0]) + across[1] + from_right(across[2])


def folded(x):
    return jnp.sum(x.reshape(-1, 8, x.shape[-1]), axis=0)


def statistics(proj, cot):
    parts = (proj, proj * proj, cot, cot * proj)
    return [jnp.sum(folded(p), axis=0, keepdims=True) for p in parts]


def pack_kernel(mw, ft, fb, ct, cb, gt, gb, head, tail):
    share = shares(mw)
    for out, fine, coarse, cot, rows in ((head, ft, ct, gt, (0, 1)), (tail, fb, cb, gb, (1, 0))):
        up = doubled(coarse[0, 0])
        for k, r in enumerate(rows):
            for c in blocks():
                act = activate(fine[0, r, :, c].astype(f32), up[:, c], share)[2]
                out[k * WIDTH : (k + 1) * WIDTH, c] = act.astype(bf16)
        out[2 * WIDTH : 3 * WIDTH] = cot[0, 0]


def factors(row, up, share):
    merged, sig, act = activate(row, up, share)
    slope = sig * (1.0 + merged * (1.0 - sig))
    return act, slope, ((row - merged) / share[2], (up - merged) / share[2])


def middle_kernel(
    mw, fine, coarse, dw, pw, cot, depth, proj, stats, partial, act, factor, slope, up
):
    share = shares(mw)
    up[...] = doubled(coarse[0].reshape(-1, CH))
    last = HEIGHT - 1
    for c in blocks():
        for i in range(HEIGHT):
            u = up[(i // 2) * WIDTH : (i // 2 + 1) * WIDTH, c]
            found = factors(fine[0, i, :, c].astype(f32), u, share)
            act[i, :, c], slope[i, :, c], (factor[0, i, :, c], factor[1, i, :, c]) = found
        for i in range(HEIGHT):
            taps = [a for a in range(3) if 0 <= i + a - 1 <= last]
            sums = convolve([act[i + a - 1, :, c] for a in taps], taps, dw, c)
            if 0 < i < last:
                depth[(i - 1) * WIDTH : i * WIDTH, c] = sums.astype(bf16)
            else:
                partial[i // last, :, c] = sums
    proj[...] = jnp.dot(depth[...], pw[...], preferred_element_type=f32)
    own = cot[0, 1:last].reshape(-1, CH).astype(f32)
    for k, s in enumerate(statistics(proj[...], own)):
        stats[k : k + 1] = s


def edge_kernel(above, below, partial, act, gt, gb, dw, pw, mid, depth, proj, stats):
    for e, (halo, a) in enumerate(((above, 0), (below, 2))):
        for c in blocks():
            near = halo[0:WIDTH, c].astype(f32)
            far = halo[WIDTH : 2 * WIDTH, c].astype(f32)
            inner = partial[e, :, c] + convolve((near,), (a,), dw, c)
            rows = (far, near, act[0, :, c]) if e == 0 else (act[HEIGHT - 1, :, c], near, far)
            outer = convolve(rows, range(3), dw, c)
            for k, row in enumerate((outer, inner) if e == 0 else (inner, outer)):
                at = (2 * e + k) * WIDTH
                depth[at : at + WIDTH, c] = row.astype(bf16)
    proj[...] = jnp.dot(depth[...], pw[...], preferred_element_type=f32)
    first = statistics(proj[WIDTH : 2 * WIDTH], gt[0, 0].astype(f32))
    last = statistics(proj[2 * WIDTH : 3 * WIDTH], gb[0, 0].astype(f32))
    whole = jnp.concatenate([x + y for x, y in zip(first, last)], axis=0) + mid[...]
    stats[...] = jnp.broadcast_to(whole[None], stats.shape)


def total_kernel(parts, out):
    out[...] = jnp.broadcast_to(jnp.sum(parts[...], axis=0)[None], out.shape)


def gradient_kernel(
    gathered, above, below, cot, pw, gain, proj_mid, proj_edge, grad_gain, grad_shift, gproj, gmap
):
    n, end = 2 * WIDTH, HEIGHT * WIDTH
    stats = jnp.sum(gathered[...], axis=0)
    mean = stats[0:1] / COUNT
    variance = stats[1:2] / COUNT - mean * mean
    inv_std = 1.0 / jnp.sqrt(variance + 1e-05)
    shift = stats[2:3]
    gained = inv_std * (stats[3:4] - mean * shift)
    grad_gain[...] = gained.reshape(CH)
    grad_shift[...] = shift.reshape(CH)
    scale = gain[...].reshape(1, CH) * inv_std
    by_proj = -(scale * inv_std * gained) / COUNT
    offset = -(scale * shift) / COUNT

    def gradient(g, p):
        return (scale * g.astype(f32) + (by_proj * (p - mean) + offset)).astype(bf16)

    gproj[0:WIDTH] = gradient(above[n : n + WIDTH], proj_edge[0:WIDTH])
    gproj[WIDTH:n] = gradient(cot[0, 0], proj_edge[WIDTH:n])
    mid_cot = cot[0, 1 : HEIGHT - 1].reshape(-1, CH)
    gproj[n:end] = gradient(mid_cot, proj_mid[...])
    gproj[end : end + WIDTH] = gradient(cot[0, HEIGHT - 1], proj_edge[n : n + WIDTH])
    gproj[end + WIDTH : end + n] = gradient(below[n : n + WIDTH], proj_edge[n + WIDTH : 2 * n])
    gmap[...] = lax.dot_general(
        gproj[...], pw[...], (((1,), (1,)), ((), ())), preferred_element_type=f32
    ).astype(bf16)


def weight_kernel(
    above, below, depth_mid, depth_edge, gproj, gmap, act, send, own_depth, point, slots
):
    n, end = 2 * WIDTH, HEIGHT * WIDTH
    own_depth[0:WIDTH] = depth_edge[WIDTH:n]
    own_depth[WIDTH : end - WIDTH] = depth_mid[...]
    own_depth[end - WIDTH : end] = depth_edge[n : n + WIDTH]
    whole_point = lax.dot_general(
        own_depth[...], gproj[WIDTH : end + WIDTH], (((0,), (0,)), ((), ())),
        preferred_element_type=f32,
    )
    zero = jnp.zeros((1, LANES), f32)
    small = [zero] * 32
    for k, c in enumerate(blocks()):
        point[k * CH : (k + 1) * CH] = whole_point[:, c]
        taps = [jnp.zeros((8, LANES), f32)] * 9
        ends = [halo[0:WIDTH, c].astype(f32) for halo in (above, below)]
        for i in range(HEIGHT):
            x = gmap[(i + 1) * WIDTH : (i + 2) * WIDTH, c].astype(f32)
            moved = from_right(x), x, from_left(x)
            for a in range(3):
                r = i + a - 1
                row = ends[0] if r < 0 else ends[1] if r == HEIGHT else act[r, :, c]
                for b in range(3):
                    taps[3 * a + b] = taps[3 * a + b] + folded(row * moved[b])
        for t in range(9):
            small[3 * t + k] = jnp.sum(taps[t], axis=0, keepdims=True)
    for s in range(32):
        slots[s, 0:PIECE] = point[s * PIECE : (s + 1) * PIECE]
        high = small[s].astype(bf16).astype(f32)
        slots[s, PIECE:SLOT] = jnp.concatenate([high, small[s] - high, zero, zero], axis=0)
    send[...] = slots[...].astype(bf16)


def level_kernel(
    mw, gmap, slope, factor, dw, grad_fine, grad_coarse, merging, moved, pairs
):
    share = shares(mw)
    m = HEIGHT * HALF // 2
    place = lax.axis_index("rows")
    keep = {
        0: jnp.where(place == 0, 0.0, 1.0),
        HEIGHT + 1: jnp.where(place == lax.axis_size("rows") - 1, 0.0, 1.0),
    }
    by_weight = [jnp.zeros((8, LANES), f32)] * 2
    for k, c in enumerate(blocks()):
        for r in range(HEIGHT + 2):
            x = gmap[r * WIDTH : (r + 1) * WIDTH, c].astype(f32)
            x = x * keep[r] if r in keep else x
            moved[0, r, :, c] = from_right(x)
            moved[1, r, :, c] = x
            moved[2, r, :, c] = from_left(x)
        for p in range(HEIGHT):
            grad_act = jnp.zeros((WIDTH, LANES), f32)
            for a in range(3):
                for b in range(3):
                    grad_act = grad_act + moved[b, p + 2 - a, :, c] * dw[a, b : b + 1, c]
            grad_merged = grad_act * slope[p, :, c]
            for t in range(2):
                by_weight[t] = by_weight[t] + folded(grad_merged * factor[t, p, :, c])
            grad_fine[0, p, :, c] = (grad_merged * share[0]).astype(bf16)
            at = 2 * k * m + (p // 2) * WIDTH
            if p % 2 == 0:
                pairs[at : at + WIDTH] = grad_merged
            else:
                pairs[at : at + WIDTH] = pairs[at : at + WIDTH] + grad_merged
        both = pairs[pl.ds(2 * k * m, m, stride=2)] + pairs[pl.ds(2 * k * m + 1, m, stride=2)]
        grad_coarse[0, :, :, c] = (both * share[1]).astype(bf16).reshape(HEIGHT // 2, HALF, LANES)
    lane = lax.broadcasted_iota(jnp.int32, (1, LANES), 1)
    first, second = [
        jnp.sum(jnp.sum(x, axis=0, keepdims=True), axis=1, keepdims=True) for x in by_weight
    ]
    merging[...] = jnp.where(lane == 0, first, jnp.where(lane == 1, second, 0.0))


def relay_kernel(parts, *refs):
    out = refs[-1]
    total = jnp.sum(parts[...].astype(f32), axis=0)
    row = lax.broadcasted_iota(jnp.int32, (SLOT, LANES), 0)
    for at in (PIECE, PIECE + 2):
        value = total[at : at + 1] + total[at + 1 : at + 2]
        if at > PIECE and len(refs) > 1:
            value = refs[0][...]
        high = value.astype(bf16).astype(f32)
        total = jnp.where(row == at, high, jnp.where(row == at + 1, value - high, total))
    out[...] = jnp.broadcast_to(total.astype(bf16)[None], out.shape)


def finish_kernel(parts, grad_point, grad_depth, grad_merging, point):
    rest, merging = [], jnp.zeros((1, LANES), f32)
    for s in range(32):
        slot = parts[s].astype(f32)
        point[s * PIECE : (s + 1) * PIECE] = slot[0:PIECE]
        rest.append(slot[PIECE : PIECE + 1] + slot[PIECE + 1 : PIECE + 2])
        merging = merging + (slot[PIECE + 2 : PIECE + 3] + slot[PIECE + 3 : PIECE + 4])
    for k, c in enumerate(blocks()):
        grad_point[:, c] = point[k * CH : (k + 1) * CH].astype(bf16)
        for t in range(9):
            grad_depth[t // 3, t % 3 : t % 3 + 1, c] = rest[3 * t + k]
    grad_merging[...] = merging[:, 0:2]


VMEM = pl.BlockSpec(memory_space=pltpu.VMEM)
SMEM = pl.BlockSpec(memory_space=pltpu.SMEM)


def call(kernel, name, outs, scratch=(), in_specs=None, cost=0, grid=(), limit=32):
    return pl.pallas_call(
        kernel,
        name=name,
        grid=grid,
        out_shape=[jax.ShapeDtypeStruct(s, t) for s, t in outs],
        in_specs=in_specs or [VMEM],
        out_specs=[VMEM] * len(outs),
        scratch_shapes=[pltpu.VMEM(s, t) for s, t in scratch],
        compiler_params=pltpu.CompilerParams(vmem_limit_bytes=limit << 20),
        cost_estimate=pl.CostEstimate(flops=cost, bytes_accessed=1 << 20, transcendentals=0),
    )


def at(shape, row):
    return pl.BlockSpec(shape, lambda i: (0, row, 0, 0))


FINE, COARSE, COT = (1, 2, WIDTH, CH), (1, 1, HALF, CH), (1, 1, WIDTH, CH)
COT_ENDS = [at(COT, 0), at(COT, HEIGHT - 1)]
FINE_ENDS = [at(FINE, 0), at(FINE, HEIGHT // 2 - 1)]
COARSE_ENDS = [at(COARSE, 0), at(COARSE, HEIGHT // 2 - 1)]


def on_device(
    fine_level, coarse_level, merging_weights, depth_weight, point_weight, norm_gain, cotangent
):
    ends = (fine_level, fine_level, coarse_level, coarse_level, cotangent, cotangent)
    head, tail = call(
        pack_kernel,
        "pack",
        [((3 * WIDTH, CH), bf16)] * 2,
        in_specs=[SMEM] + FINE_ENDS + COARSE_ENDS + COT_ENDS,
        grid=(1,),
        limit=56,
    )(merging_weights, *ends)
    n = lax.axis_size("rows")
    above = lax.ppermute(tail, "rows", [(i, i + 1) for i in range(n - 1)])
    below = lax.ppermute(head, "rows", [(i + 1, i) for i in range(n - 1)])
    whole = ((HEIGHT, WIDTH, CH), f32)
    depth_mid, proj_mid, mid, partial, act, factor, slope = call(
        middle_kernel,
        "middle",
        [
            ((MID * WIDTH, CH), bf16),
            ((MID * WIDTH, CH), f32),
            ((4, CH), f32),
            ((2, WIDTH, CH), f32),
            whole,
            ((2,) + whole[0], f32),
            whole,
        ],
        [((HEIGHT * HALF, CH), f32)],
        [SMEM] + [VMEM] * 5,
        cost=1 << 28,
    )(merging_weights, fine_level, coarse_level, depth_weight, point_weight, cotangent)
    depth_edge, proj_edge, stats = call(
        edge_kernel,
        "edge",
        [((4 * WIDTH, CH), bf16), ((4 * WIDTH, CH), f32), ((32, 4, CH), f32)],
        [],
        [VMEM] * 4 + COT_ENDS + [VMEM] * 3,
        grid=(1,),
    )(above, below, partial, act, cotangent, cotangent, depth_weight, point_weight, mid)
    (stats,) = call(total_kernel, "statistics", [((16, 4, CH), f32)])(exchange(stats, PLANE))
    rows = (((HEIGHT + 2) * WIDTH, CH), bf16)
    grad_gain, grad_shift, gproj, gmap = call(
        gradient_kernel,
        "gradient",
        [((CH,), f32), ((CH,), f32), rows, rows],
        in_specs=[VMEM] * 8,
    )(
        exchange(stats, DEPTH), above, below, cotangent, point_weight, norm_gain, proj_mid,
        proj_edge,
    )
    (send,) = call(
        weight_kernel,
        "weights",
        [((32, SLOT, LANES), bf16)],
        [
            ((HEIGHT * WIDTH, CH), bf16),
            ((3 * CH, LANES), f32),
            ((32, SLOT, LANES), f32),
        ],
        [VMEM] * 7,
    )(above, below, depth_mid, depth_edge, gproj, gmap, act)
    grad_fine, grad_coarse, merging = call(
        level_kernel,
        "levels",
        [(fine_level.shape, bf16), (coarse_level.shape, bf16), ((1, LANES), f32)],
        [((3, HEIGHT + 2, WIDTH, CH), f32), ((3 * HEIGHT * HALF, LANES), f32)],
        [SMEM] + [VMEM] * 4,
        cost=1 << 28,
        limit=56,
    )(merging_weights, gmap, slope, factor, depth_weight)
    (part,) = call(
        relay_kernel, "sum_plane", [((16, SLOT, LANES), bf16)], in_specs=[VMEM] * 2
    )(exchange(send, PLANE), merging)
    (part,) = call(relay_kernel, "sum_depth", [((32, SLOT, LANES), bf16)])(exchange(part, DEPTH))
    grad_point, grad_depth, grad_merging = call(
        finish_kernel,
        "finish",
        [((CH, CH), bf16), ((3, 3, CH), f32), ((1, 2), f32)],
        [((3 * CH, LANES), f32)],
    )(exchange(part, PLANE))
    return (
        grad_fine,
        grad_coarse,
        grad_merging.reshape(2),
        grad_depth,
        grad_point,
        grad_gain,
        grad_shift,
    )


def solution(mesh):
    split = P("dp", "rows", None, None)
    return jax.shard_map(
        on_device,
        mesh=mesh,
        in_specs=(split, split, P(), P(), P(), P(), split),
        out_specs=(split, split, P(), P(), P(), P(), P()),
        check_vma=False,
    )
```

```python
import jax
import jax.numpy as jnp
from jax import lax
from jax.experimental import pallas as pl
from jax.experimental.pallas import tpu as pltpu
from jax.sharding import PartitionSpec as P

AXES = ("dp", "rows")
COUNT = 294912
HEIGHT, WIDTH, CH, LANES = 12, 48, 384, 128
HALF = WIDTH // 2
MID = HEIGHT - 2
PIECE = 36
SLOT = 40
bf16, f32 = jnp.bfloat16, jnp.float32


def groups_of(bits):
    rest = [b for b in range(9) if b not in bits]

    def spread(value, places):
        return sum(((value >> i) & 1) << b for i, b in enumerate(places))

    return [
        [spread(r, rest) + spread(m, bits) for m in range(1 << len(bits))]
        for r in range(1 << len(rest))
    ]


PLANE = groups_of([2, 3, 4, 5, 6])
DEPTH = groups_of([0, 1, 7, 8])


def exchange(parts, groups):
    return lax.all_to_all(parts, AXES, 0, 0, axis_index_groups=groups)


def column():
    return lax.broadcasted_iota(jnp.int32, (WIDTH, LANES), 0)


def from_left(x):
    return jnp.where(column() == 0, 0.0, pltpu.roll(x, 1, 0))


def from_right(x):
    return jnp.where(column() == WIDTH - 1, 0.0, pltpu.roll(x, WIDTH - 1, 0))


def shares(weights):
    first, second = jnp.full((1, LANES), weights[0]), jnp.full((1, LANES), weights[1])
    total = first + second + 0.0001
    return first / total, second / total, total


def doubled(coarse):
    n = coarse.shape[0]
    row = lax.broadcasted_iota(jnp.int32, (2 * n, n), 0)
    place = lax.broadcasted_iota(jnp.int32, (2 * n, n), 1)
    pick = jnp.where((row == 2 * place) | (row == 2 * place + 1), 1.0, 0.0).astype(bf16)
    return jnp.dot(pick, coarse, preferred_element_type=f32)


def blocks():
    return [slice(c * LANES, (c + 1) * LANES) for c in range(CH // LANES)]


def activate(fine, up, share):
    merged = share[0] * fine + share[1] * up
    sig = jax.nn.sigmoid(merged)
    return merged, sig, (merged * sig).astype(bf16).astype(f32)


def convolve(rows, taps, dw, c):
    across = [sum(row * dw[a, b : b + 1, c] for row, a in zip(rows, taps)) for b in range(3)]
    return from_left(across[0]) + across[1] + from_right(across[2])


def folded(x):
    return jnp.sum(x.reshape(-1, 8, x.shape[-1]), axis=0)


def statistics(proj, cot):
    parts = (proj, proj * proj, cot, cot * proj)
    return [jnp.sum(folded(p), axis=0, keepdims=True) for p in parts]


def pack_kernel(mw, ft, fb, ct, cb, gt, gb, head, tail):
    share = shares(mw)
    for out, fine, coarse, cot, rows in ((head, ft, ct, gt, (0, 1)), (tail, fb, cb, gb, (1, 0))):
        up = doubled(coarse[0, 0])
        for k, r in enumerate(rows):
            for c in blocks():
                act = activate(fine[0, r, :, c].astype(f32), up[:, c], share)[2]
                out[k * WIDTH : (k + 1) * WIDTH, c] = act.astype(bf16)
        out[2 * WIDTH : 3 * WIDTH] = cot[0, 0]


def inside():
    place, end = lax.axis_index("rows"), lax.axis_size("rows") - 1
    return {0: jnp.where(place == 0, 0.0, 1.0), HEIGHT + 1: jnp.where(place == end, 0.0, 1.0)}


def factors(row, up, share):
    merged, sig, act = activate(row, up, share)
    slope = sig * (1.0 + merged * (1.0 - sig))
    scaled = slope / share[2]
    return act, slope, (scaled * (row - merged), scaled * (up - merged))


def middle_kernel(
    mw, fine, coarse, dw, pw, cot, depth, proj, stats, partial, act, weigh, slope, up, factor
):
    share = shares(mw)
    up[...] = doubled(coarse[0].reshape(-1, CH))
    last = HEIGHT - 1
    for c in blocks():
        for i in range(HEIGHT):
            u = up[(i // 2) * WIDTH : (i // 2 + 1) * WIDTH, c]
            found = factors(fine[0, i, :, c].astype(f32), u, share)
            act[i, :, c], slope[i, :, c], (factor[0, i, :, c], factor[1, i, :, c]) = found
        for i in range(HEIGHT):
            taps = [a for a in range(3) if 0 <= i + a - 1 <= last]
            sums = convolve([act[i + a - 1, :, c] for a in taps], taps, dw, c)
            if 0 < i < last:
                depth[(i - 1) * WIDTH : i * WIDTH, c] = sums.astype(bf16)
            else:
                partial[i // last, :, c] = sums
        for i in range(-1, HEIGHT + 1):
            taps = [a for a in range(3) if 0 <= i + a - 1 <= last]
            for t in range(2):
                rows = [factor[t, i + a - 1, :, c] for a in taps]
                weigh[t, i + 1, :, c] = convolve(rows, taps, dw, c)
    proj[...] = jnp.dot(depth[...], pw[...], preferred_element_type=f32)
    own = cot[0, 1:last].reshape(-1, CH).astype(f32)
    for k, s in enumerate(statistics(proj[...], own)):
        stats[k : k + 1] = s


def edge_kernel(above, below, partial, act, gt, gb, dw, pw, mid, depth, proj, stats):
    for e, (halo, a) in enumerate(((above, 0), (below, 2))):
        for c in blocks():
            near = halo[0:WIDTH, c].astype(f32)
            far = halo[WIDTH : 2 * WIDTH, c].astype(f32)
            inner = partial[e, :, c] + convolve((near,), (a,), dw, c)
            rows = (far, near, act[0, :, c]) if e == 0 else (act[HEIGHT - 1, :, c], near, far)
            outer = convolve(rows, range(3), dw, c)
            for k, row in enumerate((outer, inner) if e == 0 else (inner, outer)):
                at = (2 * e + k) * WIDTH
                depth[at : at + WIDTH, c] = row.astype(bf16)
    proj[...] = jnp.dot(depth[...], pw[...], preferred_element_type=f32)
    first = statistics(proj[WIDTH : 2 * WIDTH], gt[0, 0].astype(f32))
    last = statistics(proj[2 * WIDTH : 3 * WIDTH], gb[0, 0].astype(f32))
    whole = jnp.concatenate([x + y for x, y in zip(first, last)], axis=0) + mid[...]
    stats[...] = jnp.broadcast_to(whole[None], stats.shape)


def total_kernel(parts, out):
    out[...] = jnp.broadcast_to(jnp.sum(parts[...], axis=0)[None], out.shape)


def gradient_kernel(
    gathered, above, below, cot, pw, gain, proj_mid, proj_edge, grad_gain, grad_shift, gproj, gmap
):
    n, end = 2 * WIDTH, HEIGHT * WIDTH
    stats = jnp.sum(gathered[...], axis=0)
    mean = stats[0:1] / COUNT
    variance = stats[1:2] / COUNT - mean * mean
    inv_std = 1.0 / jnp.sqrt(variance + 1e-05)
    shift = stats[2:3]
    gained = inv_std * (stats[3:4] - mean * shift)
    grad_gain[...] = gained.reshape(CH)
    grad_shift[...] = shift.reshape(CH)
    scale = gain[...].reshape(1, CH) * inv_std
    by_proj = -(scale * inv_std * gained) / COUNT
    offset = -(scale * shift) / COUNT

    def gradient(g, p):
        return (scale * g.astype(f32) + (by_proj * (p - mean) + offset)).astype(bf16)

    gproj[0:WIDTH] = gradient(above[n : n + WIDTH], proj_edge[0:WIDTH])
    gproj[WIDTH:n] = gradient(cot[0, 0], proj_edge[WIDTH:n])
    mid_cot = cot[0, 1 : HEIGHT - 1].reshape(-1, CH)
    gproj[n:end] = gradient(mid_cot, proj_mid[...])
    gproj[end : end + WIDTH] = gradient(cot[0, HEIGHT - 1], proj_edge[n : n + WIDTH])
    gproj[end + WIDTH : end + n] = gradient(below[n : n + WIDTH], proj_edge[n + WIDTH : 2 * n])
    gmap[...] = lax.dot_general(
        gproj[...], pw[...], (((1,), (1,)), ((), ())), preferred_element_type=f32
    ).astype(bf16)


def weight_kernel(
    above, below, depth_mid, depth_edge, gproj, gmap, act, weigh, send, own_depth, point, slots
):
    n, end = 2 * WIDTH, HEIGHT * WIDTH
    own_depth[0:WIDTH] = depth_edge[WIDTH:n]
    own_depth[WIDTH : end - WIDTH] = depth_mid[...]
    own_depth[end - WIDTH : end] = depth_edge[n : n + WIDTH]
    whole_point = lax.dot_general(
        own_depth[...], gproj[WIDTH : end + WIDTH], (((0,), (0,)), ((), ())),
        preferred_element_type=f32,
    )
    zero = jnp.zeros((1, LANES), f32)
    small = [zero] * 32
    by_weight = [jnp.zeros((8, LANES), f32)] * 2
    keep = inside()
    for k, c in enumerate(blocks()):
        point[k * CH : (k + 1) * CH] = whole_point[:, c]
        taps = [jnp.zeros((8, LANES), f32)] * 9
        ends = [halo[0:WIDTH, c].astype(f32) for halo in (above, below)]
        for i in range(-1, HEIGHT + 1):
            x = gmap[(i + 1) * WIDTH : (i + 2) * WIDTH, c].astype(f32)
            x = x * keep[i + 1] if i + 1 in keep else x
            for t in range(2):
                by_weight[t] = by_weight[t] + folded(weigh[t, i + 1, :, c] * x)
            if i + 1 in keep:
                continue
            moved = from_right(x), x, from_left(x)
            for a in range(3):
                r = i + a - 1
                row = ends[0] if r < 0 else ends[1] if r == HEIGHT else act[r, :, c]
                for b in range(3):
                    taps[3 * a + b] = taps[3 * a + b] + folded(row * moved[b])
        for t in range(9):
            small[3 * t + k] = jnp.sum(taps[t], axis=0, keepdims=True)
    for t in range(2):
        small[27 + t] = jnp.sum(by_weight[t], axis=0, keepdims=True)
    for s in range(32):
        slots[s, 0:PIECE] = point[s * PIECE : (s + 1) * PIECE]
        high = small[s].astype(bf16).astype(f32)
        slots[s, PIECE:SLOT] = jnp.concatenate([high, small[s] - high, zero, zero], axis=0)
    send[...] = slots[...].astype(bf16)


def level_kernel(mw, gmap, slope, dw, grad_fine, grad_coarse, moved, pairs):
    share = shares(mw)
    m = HEIGHT * HALF // 2
    keep = inside()
    for k, c in enumerate(blocks()):
        for r in range(HEIGHT + 2):
            x = gmap[r * WIDTH : (r + 1) * WIDTH, c].astype(f32)
            x = x * keep[r] if r in keep else x
            moved[0, r, :, c] = from_right(x)
            moved[1, r, :, c] = x
            moved[2, r, :, c] = from_left(x)
        for p in range(HEIGHT):
            grad_act = jnp.zeros((WIDTH, LANES), f32)
            for a in range(3):
                for b in range(3):
                    grad_act = grad_act + moved[b, p + 2 - a, :, c] * dw[a, b : b + 1, c]
            grad_merged = grad_act * slope[p, :, c]
            grad_fine[0, p, :, c] = (grad_merged * share[0]).astype(bf16)
            at = 2 * k * m + (p // 2) * WIDTH
            if p % 2 == 0:
                pairs[at : at + WIDTH] = grad_merged
            else:
                pairs[at : at + WIDTH] = pairs[at : at + WIDTH] + grad_merged
        both = pairs[pl.ds(2 * k * m, m, stride=2)] + pairs[pl.ds(2 * k * m + 1, m, stride=2)]
        grad_coarse[0, :, :, c] = (both * share[1]).astype(bf16).reshape(HEIGHT // 2, HALF, LANES)


def relay_kernel(parts, out):
    total = jnp.sum(parts[...].astype(f32), axis=0)
    value = total[PIECE : PIECE + 1] + total[PIECE + 1 : PIECE + 2]
    high = value.astype(bf16).astype(f32)
    row = lax.broadcasted_iota(jnp.int32, (SLOT, LANES), 0)
    total = jnp.where(row == PIECE, high, jnp.where(row == PIECE + 1, value - high, total))
    out[...] = jnp.broadcast_to(total.astype(bf16)[None], out.shape)


def finish_kernel(parts, grad_point, grad_depth, grad_merging, point):
    rest = []
    for s in range(32):
        slot = parts[s].astype(f32)
        point[s * PIECE : (s + 1) * PIECE] = slot[0:PIECE]
        rest.append(slot[PIECE : PIECE + 1] + slot[PIECE + 1 : PIECE + 2])
    for k, c in enumerate(blocks()):
        grad_point[:, c] = point[k * CH : (k + 1) * CH].astype(bf16)
        for t in range(9):
            grad_depth[t // 3, t % 3 : t % 3 + 1, c] = rest[3 * t + k]
    sums = [jnp.sum(rest[27 + t], axis=1, keepdims=True) for t in range(2)]
    grad_merging[...] = jnp.concatenate(sums, axis=1)


VMEM = pl.BlockSpec(memory_space=pltpu.VMEM)
SMEM = pl.BlockSpec(memory_space=pltpu.SMEM)


def call(kernel, name, outs, scratch=(), in_specs=None, cost=0, grid=(), limit=32):
    return pl.pallas_call(
        kernel,
        name=name,
        grid=grid,
        out_shape=[jax.ShapeDtypeStruct(s, t) for s, t in outs],
        in_specs=in_specs or [VMEM],
        out_specs=[VMEM] * len(outs),
        scratch_shapes=[pltpu.VMEM(s, t) for s, t in scratch],
        compiler_params=pltpu.CompilerParams(vmem_limit_bytes=limit << 20),
        cost_estimate=pl.CostEstimate(flops=cost, bytes_accessed=1 << 20, transcendentals=0),
    )


def at(shape, row):
    return pl.BlockSpec(shape, lambda i: (0, row, 0, 0))


FINE, COARSE, COT = (1, 2, WIDTH, CH), (1, 1, HALF, CH), (1, 1, WIDTH, CH)
COT_ENDS = [at(COT, 0), at(COT, HEIGHT - 1)]
FINE_ENDS = [at(FINE, 0), at(FINE, HEIGHT // 2 - 1)]
COARSE_ENDS = [at(COARSE, 0), at(COARSE, HEIGHT // 2 - 1)]


def on_device(
    fine_level, coarse_level, merging_weights, depth_weight, point_weight, norm_gain, cotangent
):
    ends = (fine_level, fine_level, coarse_level, coarse_level, cotangent, cotangent)
    head, tail = call(
        pack_kernel,
        "pack",
        [((3 * WIDTH, CH), bf16)] * 2,
        in_specs=[SMEM] + FINE_ENDS + COARSE_ENDS + COT_ENDS,
        grid=(1,),
        limit=56,
    )(merging_weights, *ends)
    n = lax.axis_size("rows")
    above = lax.ppermute(tail, "rows", [(i, i + 1) for i in range(n - 1)])
    below = lax.ppermute(head, "rows", [(i + 1, i) for i in range(n - 1)])
    whole = ((HEIGHT, WIDTH, CH), f32)
    depth_mid, proj_mid, mid, partial, act, weigh, slope = call(
        middle_kernel,
        "middle",
        [
            ((MID * WIDTH, CH), bf16),
            ((MID * WIDTH, CH), f32),
            ((4, CH), f32),
            ((2, WIDTH, CH), f32),
            whole,
            ((2, HEIGHT + 2, WIDTH, CH), f32),
            whole,
        ],
        [((HEIGHT * HALF, CH), f32), ((2,) + whole[0], f32)],
        [SMEM] + [VMEM] * 5,
        cost=1 << 28,
    )(merging_weights, fine_level, coarse_level, depth_weight, point_weight, cotangent)
    depth_edge, proj_edge, stats = call(
        edge_kernel,
        "edge",
        [((4 * WIDTH, CH), bf16), ((4 * WIDTH, CH), f32), ((32, 4, CH), f32)],
        [],
        [VMEM] * 4 + COT_ENDS + [VMEM] * 3,
        grid=(1,),
    )(above, below, partial, act, cotangent, cotangent, depth_weight, point_weight, mid)
    (stats,) = call(total_kernel, "statistics", [((16, 4, CH), f32)])(exchange(stats, PLANE))
    rows = (((HEIGHT + 2) * WIDTH, CH), bf16)
    grad_gain, grad_shift, gproj, gmap = call(
        gradient_kernel,
        "gradient",
        [((CH,), f32), ((CH,), f32), rows, rows],
        in_specs=[VMEM] * 8,
    )(
        exchange(stats, DEPTH), above, below, cotangent, point_weight, norm_gain, proj_mid,
        proj_edge,
    )
    (send,) = call(
        weight_kernel,
        "weights",
        [((32, SLOT, LANES), bf16)],
        [
            ((HEIGHT * WIDTH, CH), bf16),
            ((3 * CH, LANES), f32),
            ((32, SLOT, LANES), f32),
        ],
        [VMEM] * 8,
    )(above, below, depth_mid, depth_edge, gproj, gmap, act, weigh)
    grad_fine, grad_coarse = call(
        level_kernel,
        "levels",
        [(fine_level.shape, bf16), (coarse_level.shape, bf16)],
        [((3, HEIGHT + 2, WIDTH, CH), f32), ((3 * HEIGHT * HALF, LANES), f32)],
        [SMEM] + [VMEM] * 3,
        cost=1 << 28,
        limit=56,
    )(merging_weights, gmap, slope, depth_weight)
    (part,) = call(relay_kernel, "sum_plane", [((16, SLOT, LANES), bf16)])(exchange(send, PLANE))
    (part,) = call(relay_kernel, "sum_depth", [((32, SLOT, LANES), bf16)])(exchange(part, DEPTH))
    grad_point, grad_depth, grad_merging = call(
        finish_kernel,
        "finish",
        [((CH, CH), bf16), ((3, 3, CH), f32), ((1, 2), f32)],
        [((3 * CH, LANES), f32)],
    )(exchange(part, PLANE))
    return (
        grad_fine,
        grad_coarse,
        grad_merging.reshape(2),
        grad_depth,
        grad_point,
        grad_gain,
        grad_shift,
    )


def solution(mesh):
    split = P("dp", "rows", None, None)
    return jax.shard_map(
        on_device,
        mesh=mesh,
        in_specs=(split, split, P(), P(), P(), P(), split),
        out_specs=(split, split, P(), P(), P(), P(), P()),
        check_vma=False,
    )
```

```python
import jax
import jax.numpy as jnp
from jax import lax
from jax.experimental import pallas as pl
from jax.experimental.pallas import tpu as pltpu
from jax.sharding import PartitionSpec as P

AXES = ("dp", "rows")
COUNT = 294912
HEIGHT, WIDTH, CH, LANES = 12, 48, 384, 128
HALF = WIDTH // 2
MID = HEIGHT - 2
PIECE = 36
SLOT = 40
bf16, f32 = jnp.bfloat16, jnp.float32


def groups_of(bits):
    rest = [b for b in range(9) if b not in bits]

    def spread(value, places):
        return sum(((value >> i) & 1) << b for i, b in enumerate(places))

    return [
        [spread(r, rest) + spread(m, bits) for m in range(1 << len(bits))]
        for r in range(1 << len(rest))
    ]


PLANE = groups_of([2, 3, 4, 5, 6])
DEPTH = groups_of([0, 1, 7, 8])


def exchange(parts, groups):
    return lax.all_to_all(parts, AXES, 0, 0, axis_index_groups=groups)


def column():
    return lax.broadcasted_iota(jnp.int32, (WIDTH, LANES), 0)


def from_left(x):
    return jnp.where(column() == 0, 0.0, pltpu.roll(x, 1, 0))


def from_right(x):
    return jnp.where(column() == WIDTH - 1, 0.0, pltpu.roll(x, WIDTH - 1, 0))


def shares(weights):
    first, second = jnp.full((1, LANES), weights[0]), jnp.full((1, LANES), weights[1])
    total = first + second + 0.0001
    return first / total, second / total, total


def doubled(coarse):
    n = coarse.shape[0]
    row = lax.broadcasted_iota(jnp.int32, (2 * n, n), 0)
    place = lax.broadcasted_iota(jnp.int32, (2 * n, n), 1)
    pick = jnp.where((row == 2 * place) | (row == 2 * place + 1), 1.0, 0.0).astype(bf16)
    return jnp.dot(pick, coarse, preferred_element_type=f32)


def blocks():
    return [slice(c * LANES, (c + 1) * LANES) for c in range(CH // LANES)]


def activate(fine, up, share):
    merged = share[0] * fine + share[1] * up
    sig = jax.nn.sigmoid(merged)
    return merged, sig, (merged * sig).astype(bf16).astype(f32)


def convolve(rows, taps, dw, c):
    across = [sum(row * dw[a, b : b + 1, c] for row, a in zip(rows, taps)) for b in range(3)]
    return from_left(across[0]) + across[1] + from_right(across[2])


def folded(x):
    return jnp.sum(x.reshape(-1, 8, x.shape[-1]), axis=0)


def statistics(proj, cot):
    parts = (proj, proj * proj, cot, cot * proj)
    return [jnp.sum(folded(p), axis=0, keepdims=True) for p in parts]


def pack_kernel(mw, fine, coarse, cot, head, tail, fines, coarses, acts, sems):
    last = HEIGHT - 1
    ends = ((head, 0, 0, 0, (0, 1)), (tail, last - 1, HEIGHT // 2 - 1, last, (1, 0)))
    loads, moves = [], []
    for e, (out, first, low, row, _) in enumerate(ends):
        loads.append(
            (
                pltpu.make_async_copy(fine.at[0, pl.ds(first, 2)], fines.at[e], sems.at[4 * e]),
                pltpu.make_async_copy(coarse.at[0, low], coarses.at[e], sems.at[4 * e + 1]),
            )
        )
        rows = out.at[pl.ds(2 * WIDTH, WIDTH)]
        moves.append(pltpu.make_async_copy(cot.at[0, row], rows, sems.at[4 * e + 2]))
    for pair in loads:
        for copy in pair:
            copy.start()
    for copy in moves:
        copy.start()
    share = shares(mw)
    for e, (out, _, _, _, order) in enumerate(ends):
        for copy in loads[e]:
            copy.wait()
        up = doubled(coarses[e])
        for k, r in enumerate(order):
            for c in blocks():
                act = activate(fines[e, r, :, c].astype(f32), up[:, c], share)[2]
                acts[e, k * WIDTH : (k + 1) * WIDTH, c] = act.astype(bf16)
        rows = out.at[pl.ds(0, 2 * WIDTH)]
        moves.append(pltpu.make_async_copy(acts.at[e], rows, sems.at[4 * e + 3]))
        moves[-1].start()
    for copy in moves:
        copy.wait()


def inside():
    place, end = lax.axis_index("rows"), lax.axis_size("rows") - 1
    return {0: jnp.where(place == 0, 0.0, 1.0), HEIGHT + 1: jnp.where(place == end, 0.0, 1.0)}


def factors(row, up, share):
    merged, sig, act = activate(row, up, share)
    slope = sig * (1.0 + merged * (1.0 - sig))
    scaled = slope / share[2]
    return act, slope, (scaled * (row - merged), scaled * (up - merged))


def middle_kernel(
    mw, fine, coarse, dw, pw, cot, depth, proj, stats, partial, act, weigh, slope, up, factor
):
    share = shares(mw)
    up[...] = doubled(coarse[0].reshape(-1, CH))
    last = HEIGHT - 1
    for c in blocks():
        for i in range(HEIGHT):
            u = up[(i // 2) * WIDTH : (i // 2 + 1) * WIDTH, c]
            found = factors(fine[0, i, :, c].astype(f32), u, share)
            act[i, :, c], slope[i, :, c], (factor[0, i, :, c], factor[1, i, :, c]) = found
        for i in range(HEIGHT):
            taps = [a for a in range(3) if 0 <= i + a - 1 <= last]
            sums = convolve([act[i + a - 1, :, c] for a in taps], taps, dw, c)
            if 0 < i < last:
                depth[(i - 1) * WIDTH : i * WIDTH, c] = sums.astype(bf16)
            else:
                partial[i // last, :, c] = sums
        for i in range(-1, HEIGHT + 1):
            taps = [a for a in range(3) if 0 <= i + a - 1 <= last]
            for t in range(2):
                rows = [factor[t, i + a - 1, :, c] for a in taps]
                weigh[t, i + 1, :, c] = convolve(rows, taps, dw, c)
    proj[...] = jnp.dot(depth[...], pw[...], preferred_element_type=f32)
    own = cot[0, 1:last].reshape(-1, CH).astype(f32)
    for k, s in enumerate(statistics(proj[...], own)):
        stats[k : k + 1] = s


def edge_kernel(above, below, partial, act, gt, gb, dw, pw, mid, depth, proj, stats):
    for e, (halo, a) in enumerate(((above, 0), (below, 2))):
        for c in blocks():
            near = halo[0:WIDTH, c].astype(f32)
            far = halo[WIDTH : 2 * WIDTH, c].astype(f32)
            inner = partial[e, :, c] + convolve((near,), (a,), dw, c)
            rows = (far, near, act[0, :, c]) if e == 0 else (act[HEIGHT - 1, :, c], near, far)
            outer = convolve(rows, range(3), dw, c)
            for k, row in enumerate((outer, inner) if e == 0 else (inner, outer)):
                at = (2 * e + k) * WIDTH
                depth[at : at + WIDTH, c] = row.astype(bf16)
    proj[...] = jnp.dot(depth[...], pw[...], preferred_element_type=f32)
    first = statistics(proj[WIDTH : 2 * WIDTH], gt[0, 0].astype(f32))
    last = statistics(proj[2 * WIDTH : 3 * WIDTH], gb[0, 0].astype(f32))
    whole = jnp.concatenate([x + y for x, y in zip(first, last)], axis=0) + mid[...]
    stats[...] = jnp.broadcast_to(whole[None], stats.shape)


def total_kernel(parts, out):
    out[...] = jnp.broadcast_to(jnp.sum(parts[...], axis=0)[None], out.shape)


def gradient_kernel(
    gathered, above, below, cot, pw, gain, proj_mid, proj_edge, grad_gain, grad_shift, gproj, gmap
):
    n, end = 2 * WIDTH, HEIGHT * WIDTH
    stats = jnp.sum(gathered[...], axis=0)
    mean = stats[0:1] / COUNT
    variance = stats[1:2] / COUNT - mean * mean
    inv_std = 1.0 / jnp.sqrt(variance + 1e-05)
    shift = stats[2:3]
    gained = inv_std * (stats[3:4] - mean * shift)
    grad_gain[...] = gained.reshape(CH)
    grad_shift[...] = shift.reshape(CH)
    scale = gain[...].reshape(1, CH) * inv_std
    by_proj = -(scale * inv_std * gained) / COUNT
    offset = -(scale * shift) / COUNT

    def gradient(g, p):
        return (scale * g.astype(f32) + (by_proj * (p - mean) + offset)).astype(bf16)

    gproj[0:WIDTH] = gradient(above[n : n + WIDTH], proj_edge[0:WIDTH])
    gproj[WIDTH:n] = gradient(cot[0, 0], proj_edge[WIDTH:n])
    mid_cot = cot[0, 1 : HEIGHT - 1].reshape(-1, CH)
    gproj[n:end] = gradient(mid_cot, proj_mid[...])
    gproj[end : end + WIDTH] = gradient(cot[0, HEIGHT - 1], proj_edge[n : n + WIDTH])
    gproj[end + WIDTH : end + n] = gradient(below[n : n + WIDTH], proj_edge[n + WIDTH : 2 * n])
    gmap[...] = lax.dot_general(
        gproj[...], pw[...], (((1,), (1,)), ((), ())), preferred_element_type=f32
    ).astype(bf16)


def weight_kernel(
    above, below, depth_mid, depth_edge, gproj, gmap, act, weigh, send, own_depth, point, slots
):
    n, end = 2 * WIDTH, HEIGHT * WIDTH
    own_depth[0:WIDTH] = depth_edge[WIDTH:n]
    own_depth[WIDTH : end - WIDTH] = depth_mid[...]
    own_depth[end - WIDTH : end] = depth_edge[n : n + WIDTH]
    whole_point = lax.dot_general(
        own_depth[...], gproj[WIDTH : end + WIDTH], (((0,), (0,)), ((), ())),
        preferred_element_type=f32,
    )
    zero = jnp.zeros((1, LANES), f32)
    small = [zero] * 32
    by_weight = [jnp.zeros((8, LANES), f32)] * 2
    keep = inside()
    for k, c in enumerate(blocks()):
        point[k * CH : (k + 1) * CH] = whole_point[:, c]
        taps = [jnp.zeros((8, LANES), f32)] * 9
        ends = [halo[0:WIDTH, c].astype(f32) for halo in (above, below)]
        for i in range(-1, HEIGHT + 1):
            x = gmap[(i + 1) * WIDTH : (i + 2) * WIDTH, c].astype(f32)
            x = x * keep[i + 1] if i + 1 in keep else x
            for t in range(2):
                by_weight[t] = by_weight[t] + folded(weigh[t, i + 1, :, c] * x)
            if i + 1 in keep:
                continue
            moved = from_right(x), x, from_left(x)
            for a in range(3):
                r = i + a - 1
                row = ends[0] if r < 0 else ends[1] if r == HEIGHT else act[r, :, c]
                for b in range(3):
                    taps[3 * a + b] = taps[3 * a + b] + folded(row * moved[b])
        for t in range(9):
            small[3 * t + k] = jnp.sum(taps[t], axis=0, keepdims=True)
    for t in range(2):
        small[27 + t] = jnp.sum(by_weight[t], axis=0, keepdims=True)
    for s in range(32):
        slots[s, 0:PIECE] = point[s * PIECE : (s + 1) * PIECE]
        high = small[s].astype(bf16).astype(f32)
        slots[s, PIECE:SLOT] = jnp.concatenate([high, small[s] - high, zero, zero], axis=0)
    send[...] = slots[...].astype(bf16)


def level_kernel(mw, gmap, slope, dw, grad_fine, grad_coarse, moved, pairs):
    share = shares(mw)
    m = HEIGHT * HALF // 2
    keep = inside()
    for k, c in enumerate(blocks()):
        for r in range(HEIGHT + 2):
            x = gmap[r * WIDTH : (r + 1) * WIDTH, c].astype(f32)
            x = x * keep[r] if r in keep else x
            moved[0, r, :, c] = from_right(x)
            moved[1, r, :, c] = x
            moved[2, r, :, c] = from_left(x)
        for p in range(HEIGHT):
            grad_act = jnp.zeros((WIDTH, LANES), f32)
            for a in range(3):
                for b in range(3):
                    grad_act = grad_act + moved[b, p + 2 - a, :, c] * dw[a, b : b + 1, c]
            grad_merged = grad_act * slope[p, :, c]
            grad_fine[0, p, :, c] = (grad_merged * share[0]).astype(bf16)
            at = 2 * k * m + (p // 2) * WIDTH
            if p % 2 == 0:
                pairs[at : at + WIDTH] = grad_merged
            else:
                pairs[at : at + WIDTH] = pairs[at : at + WIDTH] + grad_merged
        both = pairs[pl.ds(2 * k * m, m, stride=2)] + pairs[pl.ds(2 * k * m + 1, m, stride=2)]
        grad_coarse[0, :, :, c] = (both * share[1]).astype(bf16).reshape(HEIGHT // 2, HALF, LANES)


def relay_kernel(parts, out):
    total = jnp.sum(parts[...].astype(f32), axis=0)
    value = total[PIECE : PIECE + 1] + total[PIECE + 1 : PIECE + 2]
    high = value.astype(bf16).astype(f32)
    row = lax.broadcasted_iota(jnp.int32, (SLOT, LANES), 0)
    total = jnp.where(row == PIECE, high, jnp.where(row == PIECE + 1, value - high, total))
    out[...] = jnp.broadcast_to(total.astype(bf16)[None], out.shape)


def finish_kernel(parts, grad_point, grad_depth, grad_merging, point):
    rest = []
    for s in range(32):
        slot = parts[s].astype(f32)
        point[s * PIECE : (s + 1) * PIECE] = slot[0:PIECE]
        rest.append(slot[PIECE : PIECE + 1] + slot[PIECE + 1 : PIECE + 2])
    for k, c in enumerate(blocks()):
        grad_point[:, c] = point[k * CH : (k + 1) * CH].astype(bf16)
        for t in range(9):
            grad_depth[t // 3, t % 3 : t % 3 + 1, c] = rest[3 * t + k]
    sums = [jnp.sum(rest[27 + t], axis=1, keepdims=True) for t in range(2)]
    grad_merging[...] = jnp.concatenate(sums, axis=1)


VMEM = pl.BlockSpec(memory_space=pltpu.VMEM)
SMEM = pl.BlockSpec(memory_space=pltpu.SMEM)


def call(kernel, name, outs, scratch=(), in_specs=None, cost=0, grid=(), limit=32):
    return pl.pallas_call(
        kernel,
        name=name,
        grid=grid,
        out_shape=[jax.ShapeDtypeStruct(s, t) for s, t in outs],
        in_specs=in_specs or [VMEM],
        out_specs=[VMEM] * len(outs),
        scratch_shapes=[pltpu.VMEM(s, t) for s, t in scratch],
        compiler_params=pltpu.CompilerParams(vmem_limit_bytes=limit << 20),
        cost_estimate=pl.CostEstimate(flops=cost, bytes_accessed=1 << 20, transcendentals=0),
    )


def at(shape, row):
    return pl.BlockSpec(shape, lambda i: (0, row, 0, 0))


FINE, COARSE, COT = (1, 2, WIDTH, CH), (1, 1, HALF, CH), (1, 1, WIDTH, CH)
COT_ENDS = [at(COT, 0), at(COT, HEIGHT - 1)]
FINE_ENDS = [at(FINE, 0), at(FINE, HEIGHT // 2 - 1)]
COARSE_ENDS = [at(COARSE, 0), at(COARSE, HEIGHT // 2 - 1)]


def on_device(
    fine_level, coarse_level, merging_weights, depth_weight, point_weight, norm_gain, cotangent
):
    any_space = pl.BlockSpec(memory_space=pl.ANY)
    head, tail = pl.pallas_call(
        pack_kernel,
        name="pack",
        out_shape=[jax.ShapeDtypeStruct((3 * WIDTH, CH), bf16)] * 2,
        in_specs=[SMEM] + [any_space] * 3,
        out_specs=[any_space] * 2,
        scratch_shapes=[
            pltpu.VMEM((2, 2, WIDTH, CH), bf16),
            pltpu.VMEM((2, HALF, CH), bf16),
            pltpu.VMEM((2, 2 * WIDTH, CH), bf16),
            pltpu.SemaphoreType.DMA((8,)),
        ],
        compiler_params=pltpu.CompilerParams(vmem_limit_bytes=56 << 20),
    )(merging_weights, fine_level, coarse_level, cotangent)
    n = lax.axis_size("rows")
    above = lax.ppermute(tail, "rows", [(i, i + 1) for i in range(n - 1)])
    below = lax.ppermute(head, "rows", [(i + 1, i) for i in range(n - 1)])
    whole = ((HEIGHT, WIDTH, CH), f32)
    depth_mid, proj_mid, mid, partial, act, weigh, slope = call(
        middle_kernel,
        "middle",
        [
            ((MID * WIDTH, CH), bf16),
            ((MID * WIDTH, CH), f32),
            ((4, CH), f32),
            ((2, WIDTH, CH), f32),
            whole,
            ((2, HEIGHT + 2, WIDTH, CH), f32),
            whole,
        ],
        [((HEIGHT * HALF, CH), f32), ((2,) + whole[0], f32)],
        [SMEM] + [VMEM] * 5,
        cost=1 << 28,
    )(merging_weights, fine_level, coarse_level, depth_weight, point_weight, cotangent)
    depth_edge, proj_edge, stats = call(
        edge_kernel,
        "edge",
        [((4 * WIDTH, CH), bf16), ((4 * WIDTH, CH), f32), ((32, 4, CH), f32)],
        [],
        [VMEM] * 4 + COT_ENDS + [VMEM] * 3,
        grid=(1,),
    )(above, below, partial, act, cotangent, cotangent, depth_weight, point_weight, mid)
    (stats,) = call(total_kernel, "statistics", [((16, 4, CH), f32)])(exchange(stats, PLANE))
    rows = (((HEIGHT + 2) * WIDTH, CH), bf16)
    grad_gain, grad_shift, gproj, gmap = call(
        gradient_kernel,
        "gradient",
        [((CH,), f32), ((CH,), f32), rows, rows],
        in_specs=[VMEM] * 8,
    )(
        exchange(stats, DEPTH), above, below, cotangent, point_weight, norm_gain, proj_mid,
        proj_edge,
    )
    (send,) = call(
        weight_kernel,
        "weights",
        [((32, SLOT, LANES), bf16)],
        [
            ((HEIGHT * WIDTH, CH), bf16),
            ((3 * CH, LANES), f32),
            ((32, SLOT, LANES), f32),
        ],
        [VMEM] * 8,
    )(above, below, depth_mid, depth_edge, gproj, gmap, act, weigh)
    grad_fine, grad_coarse = call(
        level_kernel,
        "levels",
        [(fine_level.shape, bf16), (coarse_level.shape, bf16)],
        [((3, HEIGHT + 2, WIDTH, CH), f32), ((3 * HEIGHT * HALF, LANES), f32)],
        [SMEM] + [VMEM] * 3,
        cost=1 << 28,
        limit=56,
    )(merging_weights, gmap, slope, depth_weight)
    (part,) = call(relay_kernel, "sum_plane", [((16, SLOT, LANES), bf16)])(exchange(send, PLANE))
    (part,) = call(relay_kernel, "sum_depth", [((32, SLOT, LANES), bf16)])(exchange(part, DEPTH))
    grad_point, grad_depth, grad_merging = call(
        finish_kernel,
        "finish",
        [((CH, CH), bf16), ((3, 3, CH), f32), ((1, 2), f32)],
        [((3 * CH, LANES), f32)],
    )(exchange(part, PLANE))
    return (
        grad_fine,
        grad_coarse,
        grad_merging.reshape(2),
        grad_depth,
        grad_point,
        grad_gain,
        grad_shift,
    )


def solution(mesh):
    split = P("dp", "rows", None, None)
    return jax.shard_map(
        on_device,
        mesh=mesh,
        in_specs=(split, split, P(), P(), P(), P(), split),
        out_specs=(split, split, P(), P(), P(), P(), P()),
        check_vma=False,
    )
```
